32 devices in a mesh: dp: 8 (over z, x), head: 4 (over y, core).
Axes of the slice: x: 2, y: 2, z: 4, core: 2. Of those that a mesh axis runs over, the one named last changes fastest.
Arguments:
- residual_in: float32 [16384, 512], P(('dp', 'head')), may hold values from -6 to 6
- cotangent: float32 [16384, 512], P(('dp', 'head')), may hold values from -6 to 6
- triple_weight: bfloat16 [512, 1536], P(None, 'head'), may hold values from -0.25 to 0.25
- proj_weight: bfloat16 [512, 512], P('head'), may hold values from -1.5 to 1.5
- up_weight: bfloat16 [512, 2048], P(None, 'head'), may hold values from -0.25 to 0.25
- up_bias: bfloat16 [2048], P('head'), may hold values from -1.5 to 1.5
- down_weight: bfloat16 [2048, 512], P('head'), may hold values from -0.125 to 0.125
- proj_bias: float32 [512], replicated, may hold values from -1.5 to 1.5
- down_bias: float32 [512], replicated, may hold values from -1.5 to 1.5
- first_gain: float32 [512], replicated, may hold values from 0.5 to 1.5
- first_shift: float32 [512], replicated, may hold values from -1.5 to 1.5
- second_gain: float32 [512], replicated, may hold values from 0.5 to 1.5
- second_shift: float32 [512], replicated, may hold values from -1.5 to 1.5
- start_steps: int32 [128], P('dp'), may hold values from 0 to 20
- cond_counts: int32 [128], P('dp'), may hold values from 0 to 12
- valid_lengths: int32 [128], P('dp'), may hold values from 64 to 126
Outputs:
- block_out: float32 [16384, 512], P(('dp', 'head'))
- grad_input: float32 [16384, 512], P(('dp', 'head'))
- grad_triple: float32 [512, 1536], P(None, 'head')
- grad_proj: float32 [512, 512], P('head')
- grad_up: float32 [512, 2048], P(None, 'head')
- grad_up_bias: float32 [2048], P('head')
- grad_down: float32 [2048, 512], P('head')
- grad_proj_bias: float32 [512], replicated
- grad_down_bias: float32 [512], replicated
- grad_first_gain: float32 [512], replicated
- grad_first_shift: float32 [512], replicated
- grad_second_gain: float32 [512], replicated
- grad_second_shift: float32 [512], replicated
The draws below stay inside these ranges and needn't reach their ends.
All inputs are finite; a program needn't handle non-finite values.
Results may differ from the reference program's by a relative error of at most 0.0095.
The reference program's roundings to bfloat16 on the way count: a program that leaves them out, or rounds other values in their place, can miss the bound.
Values may be sent and summed in bfloat16 or wider, within the bound.
No kernel may reach another device: no remote copies, remote signals or barrier semaphores. Data moves between devices by JAX's collectives and lax.ppermute only.
A program may use at most 128 MiB of HBM per device.

```python
import math
import jax
import jax.numpy as jnp
from jax import lax

D = 512
HEADS = 8
HEAD_DIM = 64
FF = 2048
SEQ = 128
STEP_TOKENS = 6
SEQUENCES = 128
TOKENS = 16384


def with_ends(values, own_key, low, largest):
    shape = values.shape
    spot = [jax.random.randint(jax.random.fold_in(own_key, axis), (), 0, shape[axis]) for axis in range(len(shape))]
    values = values.at[tuple(spot)].set(low)
    longest = shape.index(max(shape))
    spot[longest] = (spot[longest] + 1) % shape[longest]
    return values.at[tuple(spot)].set(largest)


def level_of(own_key, dims, shards, least, top_value):
    level, own = 1.0, jax.random.fold_in(own_key, 6)
    for dim, parts in shards:
        heights = jnp.exp(jax.random.uniform(jax.random.fold_in(own, dim), (parts,), jnp.float32, least / len(shards), top_value / len(shards)))
        level = level * jnp.repeat(heights, dims[dim] // parts).reshape([-1 if axis == dim else 1 for axis in range(len(dims))])
    return level


def normal_values(key, shape, scale, reach, shards=(), held_as=jnp.bfloat16):
    level = level_of(key, shape, shards, -0.22, 0.18) if shards else 1.0
    result = jax.random.normal(key, shape, jnp.float32) * scale * level
    return jnp.minimum(jnp.maximum(result, -reach), reach).astype(held_as)


def setup_inputs(seed: int = 0) -> dict:
    splits = jax.random.split(jax.random.key(seed), 17)
    residual_in = normal_values(splits[0], (TOKENS, D), 1.0, 6.0, ((0, 32),), jnp.float32)
    cotangent = normal_values(splits[1], (TOKENS, D), 1.0, 6.0, ((0, 32),), jnp.float32)
    triple_weight = normal_values(splits[2], (D, 3 * D), D ** -0.5, 0.25, ((1, 4),))
    proj_weight = normal_values(splits[3], (D, D), (D // 32) ** -0.5, 1.5, ((0, 4),))
    up_weight = normal_values(splits[4], (D, FF), D ** -0.5, 0.25, ((1, 4),))
    up_bias = normal_values(splits[5], (FF,), 0.3, 1.5, ((0, 4),))
    down_weight = normal_values(splits[6], (FF, D), FF ** -0.5, 0.125, ((0, 4),))
    proj_bias = normal_values(splits[7], (D,), 0.3, 1.5, (), jnp.float32)
    down_bias = normal_values(splits[8], (D,), 0.3, 1.5, (), jnp.float32)
    first_gain = jnp.clip(1.0 + 0.1 * jax.random.normal(splits[9], (D,), jnp.float32), 0.5, 1.5)
    first_shift = normal_values(splits[10], (D,), 0.3, 1.5, (), jnp.float32)
    second_gain = jnp.clip(1.0 + 0.1 * jax.random.normal(splits[11], (D,), jnp.float32), 0.5, 1.5)
    second_shift = normal_values(splits[12], (D,), 0.3, 1.5, (), jnp.float32)
    start_steps = with_ends(jax.random.randint(splits[13], (SEQUENCES,), 0, 21), jax.random.fold_in(splits[13], 1), 0, 20).astype(jnp.int32)
    cond_counts = with_ends(jax.random.randint(splits[14], (SEQUENCES,), 0, 13), jax.random.fold_in(splits[14], 1), 0, 12).astype(jnp.int32)
    valid_lengths = with_ends(jax.random.randint(splits[15], (SEQUENCES,), 64, SEQ - 1), jax.random.fold_in(splits[15], 1), 64, (SEQ - 1) - 1).astype(jnp.int32)
    return dict(residual_in=residual_in, cotangent=cotangent, triple_weight=triple_weight, proj_weight=proj_weight, up_weight=up_weight, up_bias=up_bias, down_weight=down_weight, proj_bias=proj_bias, down_bias=down_bias, first_gain=first_gain, first_shift=first_shift, second_gain=second_gain, second_shift=second_shift, start_steps=start_steps, cond_counts=cond_counts, valid_lengths=valid_lengths)


EPSILON = 1e-05
HIGH = lax.Precision.HIGHEST

@jax.custom_vjp
def low(v):
    return lax.optimization_barrier(v.astype(jnp.bfloat16)).astype(jnp.float32)

@jax.custom_vjp
def low_back(v):
    return v

def low_keep(v):
    return (low(v), None)

def low_pass(kept, grad):
    return (grad,)

def back_keep(v):
    return (v, None)

def back_low(kept, grad):
    return (low(grad),)
low.defvjp(low_keep, low_pass)
low_back.defvjp(back_keep, back_low)

def normalize(rows, gain, shift):
    centre = rows - lax.optimization_barrier(jnp.mean(rows, axis=-1, keepdims=True))
    spread = lax.optimization_barrier(jnp.mean(centre * centre, axis=-1, keepdims=True))
    return centre * lax.rsqrt(spread + EPSILON) * gain + shift

def visible(starts, counts, lengths):
    places = jnp.arange(SEQ, dtype=jnp.int32)
    groups = jnp.maximum((places // STEP_TOKENS)[None, :], starts[:, None])
    causal = groups[:, None, :] <= groups[:, :, None]
    prefix = places[None, None, :] < counts[:, None, None]
    present = places[None, None, :] < lengths[:, None, None]
    return present & (causal | prefix)

def attend_block(triple, allowed):
    shaped = triple.reshape(triple.shape[0], SEQ, HEADS, 3, HEAD_DIM)
    queries = shaped[:, :, :, 0]
    keys_all = shaped[:, :, :, 1]
    values = shaped[:, :, :, 2]
    scores = jnp.einsum('snhe,smhe->shnm', queries, keys_all, precision=HIGH) * HEAD_DIM ** (-0.5)
    scores = low_back(scores)
    scores = jnp.where(allowed[:, None], scores, -1e+30)
    top = lax.optimization_barrier(jnp.max(scores, axis=-1, keepdims=True))
    weights = jnp.exp(scores - top)
    probs = low(weights / lax.optimization_barrier(jnp.sum(weights, axis=-1, keepdims=True)))
    mixed = jnp.einsum('shnm,smhe->snhe', probs, values, precision=HIGH)
    return mixed.reshape(triple.shape[0], SEQ, D)

def forward(residual, triple_weight, proj_weight, up_weight, up_bias, down_weight, proj_bias, down_bias, first_gain, first_shift, second_gain, second_shift, allowed):
    first_rows = low(normalize(residual, first_gain, first_shift))
    triple = low(low_back(jnp.dot(first_rows, triple_weight, precision=HIGH)))
    count = math.gcd(SEQUENCES, 32)
    pieces = triple.reshape(SEQUENCES // count, count, SEQ, 3 * D)
    masks = allowed.reshape(SEQUENCES // count, count, SEQ, SEQ)
    mixed = lax.map(jax.checkpoint(lambda item: attend_block(item[0], item[1])), (pieces, masks))
    mixed = low_back(low(mixed.reshape(TOKENS, D)))
    middle = residual + low_back(jnp.dot(mixed, proj_weight, precision=HIGH)) + proj_bias
    second_rows = low(normalize(middle, second_gain, second_shift))
    up_pre = low_back(jnp.dot(second_rows, up_weight, precision=HIGH) + up_bias)
    act = low(jax.nn.gelu(up_pre))
    return middle + low_back(jnp.dot(act, down_weight, precision=HIGH)) + down_bias

def reference(residual_in, cotangent, triple_weight, proj_weight, up_weight, up_bias, down_weight, proj_bias, down_bias, first_gain, first_shift, second_gain, second_shift, start_steps, cond_counts, valid_lengths):
    allowed = visible(start_steps, cond_counts, valid_lengths)
    floats = (residual_in, triple_weight.astype(jnp.float32), proj_weight.astype(jnp.float32), up_weight.astype(jnp.float32), up_bias.astype(jnp.float32), down_weight.astype(jnp.float32), proj_bias, down_bias, first_gain, first_shift, second_gain, second_shift)

    def closed(*values):
        return forward(*values, allowed)
    block_out, pullback = jax.vjp(closed, *floats)
    grads = pullback(cotangent)
    return (block_out, grads[0], grads[1], grads[2], grads[3], grads[4], grads[5], grads[6], grads[7], grads[8], grads[9], grads[10], grads[11])
```

```python
import jax
import jax.numpy as jnp
from jax import lax
from jax.sharding import PartitionSpec as P

HEAD_DIM = 64
SEQ = 128
STEP_TOKENS = 6
EPSILON = 1e-05
NEG_FILL = -1e30
BF = jnp.bfloat16
F32 = jnp.float32
AXES = ("dp", "head")


def normalize(rows, gain, shift):
    centre = rows - jnp.mean(rows, axis=-1, keepdims=True)
    spread = jnp.mean(centre * centre, axis=-1, keepdims=True)
    return centre * lax.rsqrt(spread + EPSILON) * gain + shift


def visible(starts, counts, lengths):
    places = jnp.arange(SEQ, dtype=jnp.int32)
    groups = jnp.maximum((places // STEP_TOKENS)[None, :], starts[:, None])
    causal = groups[:, None, :] <= groups[:, :, None]
    prefix = places[None, None, :] < counts[:, None, None]
    present = places[None, None, :] < lengths[:, None, None]
    return present & (causal | prefix)


def split_triple(triple_low, heads):
    shaped = triple_low.reshape(triple_low.shape[0] // SEQ, SEQ, heads, 3, HEAD_DIM)
    return (shaped[:, :, :, 0], shaped[:, :, :, 1], shaped[:, :, :, 2])


def masked_scores(queries, keys_all, allowed):
    scores = jnp.einsum(
        "snhe,smhe->shnm", queries, keys_all, preferred_element_type=F32
    ) * HEAD_DIM ** (-0.5)
    return jnp.where(allowed[:, None], scores, NEG_FILL)


def attend_forward(triple_low, allowed, heads):
    queries, keys_all, values = split_triple(triple_low, heads)
    scores = masked_scores(queries, keys_all, allowed)
    top = jnp.max(scores, axis=-1, keepdims=True)
    weights = jnp.exp(scores - top)
    total = jnp.sum(weights, axis=-1, keepdims=True)
    probs = weights / total
    mixed = jnp.einsum("shnm,smhe->snhe", probs.astype(BF), values, preferred_element_type=F32)
    return mixed.reshape(triple_low.shape[0], heads * HEAD_DIM).astype(BF), probs


def attend_backward(triple_low, grad_mixed, probs, heads):
    queries, keys_all, values = split_triple(triple_low, heads)
    grad_heads = grad_mixed.reshape(queries.shape)
    grad_probs = jnp.einsum("snhe,smhe->shnm", grad_heads, values, preferred_element_type=F32)
    inner = jnp.sum(grad_probs * probs, axis=-1, keepdims=True)
    grad_scores = (probs * (grad_probs - inner)).astype(BF)
    factor = HEAD_DIM ** (-0.5)
    grad_queries = (
        jnp.einsum("shnm,smhe->snhe", grad_scores, keys_all, preferred_element_type=F32) * factor
    )
    grad_keys = (
        jnp.einsum("shnm,snhe->smhe", grad_scores, queries, preferred_element_type=F32) * factor
    )
    grad_values = jnp.einsum(
        "shnm,snhe->smhe", probs.astype(BF), grad_heads, preferred_element_type=F32
    )
    stacked = jnp.stack([grad_queries, grad_keys, grad_values], axis=3)
    return stacked.reshape(triple_low.shape[0], heads * 3 * HEAD_DIM).astype(BF)


class Links:
    def __init__(self, mesh):
        self.dp, self.head = mesh.shape["dp"], mesh.shape["head"]

    def swap(self, value, bit):
        total = self.dp * self.head
        return lax.ppermute(value, AXES, [(i, i ^ bit) for i in range(total)])

    def gather(self, shard):
        slots = shard[None]
        bit = self.head // 2
        while bit:
            slots = jnp.concatenate([slots, self.swap(slots, bit)], 0)
            bit //= 2
        return slots

    def scatter(self, slots):
        bit = 1
        while bit < self.head:
            half = slots.shape[0] // 2
            got = self.swap(slots[half:].astype(BF), bit)
            slots = slots[:half] + got.astype(F32)
            bit *= 2
        return slots[0]

    def total(self, part):
        place = lax.axis_index("dp")
        bit, kept = 1, []
        while bit < self.dp:
            half = part.shape[0] // 2
            mine = (place // bit) % 2
            keep = lax.dynamic_slice_in_dim(part, mine * half, half, 0)
            send = lax.dynamic_slice_in_dim(part, (1 - mine) * half, half, 0)
            part = keep + self.swap(send.astype(BF), bit * self.head).astype(F32)
            bit *= 2
        low = part.astype(BF)
        while bit > 1:
            bit //= 2
            mine = (place // bit) % 2
            other = self.swap(low, bit * self.head)
            low = jnp.where(
                mine == 0, jnp.concatenate([low, other], 0), jnp.concatenate([other, low], 0)
            )
        return low.astype(F32)

    def everywhere(self, vec, axes_bits):
        for bit in axes_bits:
            vec = vec + self.swap(vec, bit)
        return vec


def make(mesh):
    links = Links(mesh)

    def columns(slots):
        return jnp.concatenate(list(slots), 1)

    def rows_of(slots):
        return slots.reshape(-1, slots.shape[-1])

    def shards(
        residual_in,
        cotangent,
        triple_weight,
        proj_weight,
        up_weight,
        up_bias,
        down_weight,
        proj_bias,
        down_bias,
        first_gain,
        first_shift,
        second_gain,
        second_shift,
        start_steps,
        cond_counts,
        valid_lengths,
    ):
        rows = residual_in.shape[0]
        seqs = rows // SEQ
        nslots = links.head
        place = lax.axis_index("head")
        pick = lambda a: lax.dynamic_slice_in_dim(a, place * seqs, seqs, 0)
        allowed = visible(pick(start_steps), pick(cond_counts), pick(valid_lengths))
        triple_use = columns(links.gather(triple_weight))
        proj_use = rows_of(links.gather(proj_weight))
        up_use = columns(links.gather(up_weight))
        upbias_use = links.gather(up_bias[None]).reshape(-1)
        down_use = rows_of(links.gather(down_weight))
        heads = triple_use.shape[1] // (3 * HEAD_DIM)
        first_rows = normalize(residual_in, first_gain, first_shift).astype(BF)
        triple_low = jnp.dot(first_rows, triple_use, preferred_element_type=F32).astype(BF)
        mixed_low, probs = attend_forward(triple_low, allowed, heads)
        attn_out = jnp.dot(mixed_low, proj_use, preferred_element_type=F32)
        middle = residual_in + attn_out + proj_bias
        second_rows = normalize(middle, second_gain, second_shift).astype(BF)
        up_pre = jnp.dot(second_rows, up_use, preferred_element_type=F32) + upbias_use.astype(F32)
        act_low = jax.nn.gelu(up_pre).astype(BF)
        out_rows = cotangent.astype(BF)
        grad_down = jnp.einsum("nf,nd->fd", act_low, out_rows, preferred_element_type=F32)
        grad_down = links.total(links.scatter(grad_down.reshape(nslots, -1, grad_down.shape[1])))
        grad_act = jnp.einsum("nd,fd->nf", out_rows, down_use, preferred_element_type=F32)
        gelu_back = jax.vjp(jax.nn.gelu, up_pre)[1]
        grad_pre = gelu_back(grad_act)[0].astype(BF)
        grad_upbias = jnp.sum(grad_pre.astype(F32), axis=0)
        grad_up = jnp.einsum("nd,nf->df", second_rows, grad_pre, preferred_element_type=F32)
        split = lambda g: jnp.stack(jnp.split(g, nslots, axis=1))
        grad_up = links.total(links.scatter(split(grad_up)))
        grad_upbias = links.everywhere(
            links.scatter(grad_upbias.reshape(nslots, 1, -1)),
            [links.head * 2**k for k in range(links.dp.bit_length() - 1)],
        )[0]
        grad_second = jnp.einsum("nf,df->nd", grad_pre, up_use, preferred_element_type=F32)
        mlp_out = jnp.dot(act_low, down_use, preferred_element_type=F32)
        block_out = middle + mlp_out + down_bias
        second_back = jax.vjp(normalize, middle, second_gain, second_shift)[1]
        middle_rows, second_gain_part, second_shift_part = second_back(grad_second)
        grad_middle = cotangent + middle_rows
        middle_low = grad_middle.astype(BF)
        grad_proj = jnp.einsum("nh,nd->hd", mixed_low, middle_low, preferred_element_type=F32)
        grad_proj = links.total(links.scatter(grad_proj.reshape(nslots, -1, grad_proj.shape[1])))
        grad_mixed = jnp.einsum(
            "nd,hd->nh", middle_low, proj_use, preferred_element_type=F32
        ).astype(BF)
        grad_triple_low = attend_backward(triple_low, grad_mixed, probs, heads)
        grad_triple = jnp.einsum(
            "nd,nt->dt", first_rows, grad_triple_low, preferred_element_type=F32
        )
        grad_triple = links.total(links.scatter(split(grad_triple)))
        grad_first = jnp.einsum(
            "nt,dt->nd", grad_triple_low, triple_use, preferred_element_type=F32
        )
        first_back = jax.vjp(normalize, residual_in, first_gain, first_shift)[1]
        input_rows, first_gain_part, first_shift_part = first_back(grad_first)
        grad_input = grad_middle + input_rows
        sums = jnp.stack(
            [
                jnp.sum(grad_middle, axis=0),
                jnp.sum(cotangent, axis=0),
                first_gain_part,
                first_shift_part,
                second_gain_part,
                second_shift_part,
                jnp.zeros_like(first_gain_part),
                jnp.zeros_like(first_gain_part),
            ]
        )
        sums = links.everywhere(
            sums, [2**k for k in range((links.dp * links.head).bit_length() - 1)]
        )
        return (
            block_out,
            grad_input,
            grad_triple,
            grad_proj,
            grad_up,
            grad_upbias,
            grad_down,
            sums[0],
            sums[1],
            sums[2],
            sums[3],
            sums[4],
            sums[5],
        )

    return shards


def solution(mesh):
    in_specs = (
        P(("dp", "head"), None),
        P(("dp", "head"), None),
        P(None, "head"),
        P("head", None),
        P(None, "head"),
        P("head"),
        P("head", None),
        P(),
        P(),
        P(),
        P(),
        P(),
        P(),
        P("dp"),
        P("dp"),
        P("dp"),
    )
    out_specs = (
        P(("dp", "head"), None),
        P(("dp", "head"), None),
        P(None, "head"),
        P("head", None),
        P(None, "head"),
        P("head"),
        P("head", None),
        P(),
        P(),
        P(),
        P(),
        P(),
        P(),
    )
    return jax.shard_map(
        make(mesh), mesh=mesh, in_specs=in_specs, out_specs=out_specs, check_vma=False
    )
```

```python
import functools

import jax
import jax.numpy as jnp
from jax import lax
from jax.experimental import pallas as pl
from jax.experimental.pallas import tpu as pltpu
from jax.sharding import PartitionSpec as P

HEAD_DIM = 64
SEQ = 128
EPSILON = 1e-05
NEG_FILL = -1e30
BF = jnp.bfloat16
F32 = jnp.float32
AXES = ("dp", "head")
CHUNK = 128
VMEM_LIMIT = 8 * 2**20


def nn(a, b):
    return lax.dot_general(a, b, (((1,), (0,)), ((), ())), preferred_element_type=F32)


def nt(a, b):
    return lax.dot_general(a, b, (((1,), (1,)), ((), ())), preferred_element_type=F32)


def tn(a, b):
    return lax.dot_general(a, b, (((0,), (0,)), ((), ())), preferred_element_type=F32)


class Kernels:
    def __init__(self):
        self.token = jnp.zeros((8, 128), F32)

    def call(self, body, outs, *args, scalars=0, scratch=(), name=None):
        vmem = pl.BlockSpec(memory_space=pltpu.VMEM)
        smem = pl.BlockSpec(memory_space=pltpu.SMEM)
        plain, count = len(args) - scalars, len(args)

        last = count + 1 + len(outs)

        def ordered(*refs):
            refs[last][...] = refs[count][...]
            body(*refs[:count], *refs[count + 1 : last], *refs[last + 1 :])

        got = pl.pallas_call(
            ordered,
            out_shape=[jax.ShapeDtypeStruct(*out[:2]) for out in outs]
            + [jax.ShapeDtypeStruct((8, 128), F32)],
            in_specs=[vmem] * plain + [smem] * scalars + [vmem],
            out_specs=[vmem] * (len(outs) + 1),
            compiler_params=pltpu.CompilerParams(vmem_limit_bytes=VMEM_LIMIT),
            scratch_shapes=[pltpu.VMEM(*s) for s in scratch],
            cost_estimate=pl.CostEstimate(flops=0, bytes_accessed=0, transcendentals=0),
            name=name,
        )(*args, self.token)
        self.token = got[-1]
        return got[:-1]


def centred(rows):
    centre = rows - jnp.mean(rows, axis=-1, keepdims=True)
    spread = jnp.mean(centre * centre, axis=-1, keepdims=True)
    rstd = lax.rsqrt(spread + EPSILON)
    return centre * rstd, rstd


def norm_back(grad, rows, gain):
    xhat, rstd = centred(rows)
    q = grad * gain
    inner = jnp.mean(q * xhat, axis=-1, keepdims=True)
    row = rstd * (q - jnp.mean(q, axis=-1, keepdims=True) - xhat * inner)
    return row, jnp.sum(grad * xhat, axis=0, keepdims=True), jnp.sum(grad, axis=0, keepdims=True)


def prep_kernel(res, cot, gain, shift, first, first_t, out_low, out_t):
    for r in range(0, res.shape[0], CHUNK):
        xhat, _ = centred(res[r : r + CHUNK, :])
        low = (xhat * gain[...] + shift[...]).astype(BF)
        first[r : r + CHUNK, :] = low
        first_t[:, r : r + CHUNK] = low.T
        low = cot[r : r + CHUNK, :].astype(BF)
        out_low[r : r + CHUNK, :] = low
        out_t[:, r : r + CHUNK] = low.T


def lanes_low(shape):
    return lax.broadcasted_iota(jnp.int32, shape, 1) < HEAD_DIM


def half_turn(block):
    return jnp.concatenate([block[:, HEAD_DIM:], block[:, :HEAD_DIM]], 1)


def mask_of(start, count, length):
    m = lax.broadcasted_iota(jnp.int32, (SEQ, SEQ), 0)
    n = lax.broadcasted_iota(jnp.int32, (SEQ, SEQ), 1)
    group_m = jnp.maximum((m * 43) >> 8, start)
    group_n = jnp.maximum((n * 43) >> 8, start)
    return (m < length) & ((group_m <= group_n) | (m < count))


def attend(first, weight, triple, probs, mixed, scalars, seqs):
    low = lanes_low((SEQ, 2 * HEAD_DIM))
    zero = jnp.zeros((SEQ, 2 * HEAD_DIM), BF)
    triple[...] = nn(first[...], weight[...]).astype(BF)
    base, starts, counts, lengths = scalars
    for s in range(seqs):
        at = slice(s * SEQ, (s + 1) * SEQ)
        b0, b1, b2 = (triple[at, c * 128 : (c + 1) * 128] for c in range(3))
        seen = mask_of(*(ref[base + s] for ref in (starts, counts, lengths)))
        pairs = (
            (jnp.where(low, half_turn(b0), zero), b0, jnp.where(low, b1, zero)),
            (jnp.where(low, b2, zero), half_turn(b1), jnp.where(low, zero, b2)),
        )
        out = None
        for h, (keys, queries, values) in enumerate(pairs):
            score = jnp.where(seen, nt(keys, queries) * HEAD_DIM**-0.5, NEG_FILL)
            weights = jnp.exp(score - jnp.max(score, axis=0, keepdims=True))
            prob = weights * (1.0 / jnp.sum(weights, axis=0, keepdims=True))
            probs[2 * s + h] = prob
            part = tn(prob.astype(BF), values)
            out = part if out is None else out + part
        mixed[at, :] = out.astype(BF)


def attend_back(middle_low, proj, triple, probs, seqs, gtl, grad_mixed):
    low = lanes_low((SEQ, 2 * HEAD_DIM))
    zero = jnp.zeros((SEQ, 2 * HEAD_DIM), BF)
    factor = HEAD_DIM**-0.5
    grad_mixed[...] = nt(middle_low[...], proj[: 2 * HEAD_DIM, :]).astype(BF)
    for s in range(seqs):
        at = slice(s * SEQ, (s + 1) * SEQ)
        b0, b1, b2 = (triple[at, c * 128 : (c + 1) * 128] for c in range(3))
        r0, r1, r2 = (half_turn(b) for b in (b0, b1, b2))
        gm = grad_mixed[at, :]
        grads = []
        for h, values in enumerate((jnp.where(low, b1, zero), jnp.where(low, zero, b2))):
            prob = probs[2 * s + h]
            grad_prob = nt(values, gm)
            inner = jnp.sum(grad_prob * prob, axis=0, keepdims=True)
            grads.append(((prob * (grad_prob - inner)).astype(BF), prob.astype(BF)))
        (ds0, p0), (ds1, p1) = grads
        gtl[at, 0:128] = (jnp.where(low, tn(ds0, r0), nn(ds0, r0)) * factor).astype(BF)
        gtl[at, 128:256] = jnp.where(low, nn(p0, gm), tn(ds1, r2) * factor).astype(BF)
        gtl[at, 256:384] = jnp.where(low, nn(ds1, r1) * factor, nn(p1, gm)).astype(BF)


def gelu_parts(x):
    c0, c1 = 0.7978845608028654, 0.044715
    square = x * x
    t = jnp.tanh(x * (c0 + (c0 * c1) * square))
    h = 0.5 * (1.0 + t)
    slope = h + (0.5 * x) * (1.0 - t * t) * (c0 + (3.0 * c0 * c1) * square)
    return x * h, slope


def pack_kernel(proj, bias, place, base, out):
    rows, span = proj.shape[0], bias.shape[1]
    out[:rows, :] = proj[...]
    if span < out.shape[1]:
        out[rows:, :] = jnp.zeros((out.shape[0] - rows, out.shape[1]), out.dtype)
    out[rows:, :span] = jnp.broadcast_to(bias[...], (out.shape[0] - rows, span))


def pair_kernel(axis, span, *refs):
    out = refs[-1]
    for k, part in enumerate(refs[:-1]):
        if axis == 0:
            out[k * span : (k + 1) * span, :] = part[:span, :]
        else:
            out[:, k * span : (k + 1) * span] = part[:, :span]


def relay_kernel(value, out):
    out[...] = value[...]


def attend_kernel(units, seqs, *refs):
    refs = list(refs)
    take = lambda n: [refs.pop(0) for _ in range(n)]
    (first,) = take(1)
    weights = take(units)
    scalars = take(4)
    scalars = [scalars[0][0]] + scalars[1:]
    triples, probs, mixeds = take(units), take(units), take(units)
    for u in range(units):
        attend(first, weights[u], triples[u], probs[u], mixeds[u], scalars, seqs)


def project_kernel(units, *refs):
    mixeds, projs, acc = refs[:units], refs[units : 2 * units], refs[2 * units]
    acc[...] = sum(nn(mixeds[u][...], projs[u][: 2 * HEAD_DIM, :]) for u in range(units))


def second_kernel(units, *refs):
    refs = list(refs)
    take = lambda n: [refs.pop(0) for _ in range(n)]
    mixeds, projs = take(units), take(units)
    acc, residual, bias, gain, shift, middle, second, second_t = refs
    for r in range(0, acc.shape[0], CHUNK):
        at = slice(r, r + CHUNK)
        out = acc[at, :] + sum(
            nn(mixeds[u][at, :], projs[u][: 2 * HEAD_DIM, :]) for u in range(units)
        )
        out = residual[at, :] + out + bias[...]
        middle[at, :] = out
        xhat, _ = centred(out)
        low = (xhat * gain[...] + shift[...]).astype(BF)
        second[at, :] = low
        second_t[:, at] = low.T


def hidden_kernel(slots, *refs):
    refs = list(refs)
    take = lambda n: [refs.pop(0) for _ in range(n)]
    second, out_t = take(2)
    ups, biases = take(slots), take(slots)
    acts, slopes, grads = take(slots), take(slots), take(slots)
    for j in range(slots):
        bias = biases[j][-1:, : ups[j].shape[1]].astype(F32)
        for r in range(0, second.shape[0], 2 * CHUNK):
            at = slice(r, r + 2 * CHUNK)
            act, slope = gelu_parts(nn(second[at, :], ups[j][...]) + bias)
            acts[j][at, :] = act.astype(BF)
            slopes[j][at, :] = slope
        grads[j][...] = nn(out_t[...], acts[j][...]).astype(grads[j].dtype)


def hidden_back_kernel(slots, first_call, *refs):
    refs = list(refs)
    take = lambda n: [refs.pop(0) for _ in range(n)]
    out_low, second_t = take(2)
    ups, downs, slopes = take(slots), take(slots), take(slots)
    acc_in = None if first_call else take(1)[0]
    grads, biases = take(slots), take(slots)
    (acc,) = take(1)
    pre = take(slots)
    for j in range(slots):
        total = 0.0
        for r in range(0, out_low.shape[0], 2 * CHUNK):
            at = slice(r, r + 2 * CHUNK)
            low = (nt(out_low[at, :], downs[j][...]) * slopes[j][at, :]).astype(BF)
            pre[j][at, :] = low
            total = total + jnp.sum(low.astype(F32), axis=0, keepdims=True)
        biases[j][...] = total
        grads[j][...] = nn(second_t[...], pre[j][...]).astype(grads[j].dtype)
    for r in range(0, out_low.shape[0], 2 * CHUNK):
        at = slice(r, r + 2 * CHUNK)
        out = sum(nt(pre[j][at, :], ups[j][...]) for j in range(slots))
        acc[at, :] = out if first_call else acc_in[at, :] + out


def middle_kernel(grad_second, middle, gain, cot, grad_middle, middle_low, middle_t, sums):
    totals = [0.0, 0.0, 0.0]
    for r in range(0, cot.shape[0], CHUNK):
        at = slice(r, r + CHUNK)
        row, dgain, dshift = norm_back(grad_second[at, :], middle[at, :], gain[...])
        grad = cot[at, :] + row
        grad_middle[at, :] = grad
        low = grad.astype(BF)
        middle_low[at, :] = low
        middle_t[:, at] = low.T
        parts = (jnp.sum(grad, axis=0, keepdims=True), dgain, dshift)
        totals = [t + p for t, p in zip(totals, parts)]
    for i, t in enumerate(totals):
        sums[i : i + 1, :] = t


def attend_back_kernel(units, group, seqs, *refs):
    refs = list(refs)
    take = lambda n: [refs.pop(0) for _ in range(n)]
    middle_low, middle_t, first_t = take(3)
    projs, triples, probs, mixeds = take(units), take(units), take(units), take(units)
    gtls, grads, grad_mixed = take(units), take(units * group), take(units)
    heads = 2 // group
    for u in range(units):
        attend_back(middle_low, projs[u], triples[u], probs[u], seqs, gtls[u], grad_mixed[u])
        triple_grad = nn(first_t[...], gtls[u][...])
        proj_grad = nn(middle_t[...], mixeds[u][...])
        for k in range(group):
            out, span, small = grads[u * group + k], 3 * HEAD_DIM * heads, HEAD_DIM * heads
            out[:, :span] = triple_grad[:, k * span : (k + 1) * span].astype(out.dtype)
            out[:, span:] = proj_grad[:, k * small : (k + 1) * small].astype(out.dtype)


def input_kernel(units, *refs):
    refs = list(refs)
    take = lambda n: [refs.pop(0) for _ in range(n)]
    gtls, weights = take(units), take(units)
    residual, gain, grad_middle, cot = take(4)
    grad_input, sums = take(2)
    totals = [0.0, 0.0, 0.0]
    for r in range(0, cot.shape[0], CHUNK):
        at = slice(r, r + CHUNK)
        grad = sum(nt(gtls[u][at, :], weights[u][...]) for u in range(units))
        row, dgain, dshift = norm_back(grad, residual[at, :], gain[...])
        grad_input[at, :] = grad_middle[at, :] + row
        parts = (jnp.sum(cot[at, :], axis=0, keepdims=True), dgain, dshift)
        totals = [t + p for t, p in zip(totals, parts)]
    for i, t in enumerate(totals):
        sums[i : i + 1, :] = t


def output_kernel(slots, *refs):
    acts, downs = refs[:slots], refs[slots : 2 * slots]
    middle, bias, out = refs[2 * slots :]
    for r in range(0, middle.shape[0], 2 * CHUNK):
        at = slice(r, r + 2 * CHUNK)
        total = sum(nn(acts[j][at, :], downs[j][...]) for j in range(slots))
        out[at, :] = middle[at, :] + total + bias[...]


def total(terms):
    out = terms[0]
    for term in terms[1:]:
        out = out + term
    return out


def read(refs, spots, at):
    return total([refs[i][pl.ds(first + at[0], at[1]), :].astype(F32) for i, first in spots])


def send_kernel(spots, rows, *refs):
    out = refs[-1]
    for k, spot in enumerate(spots):
        out[k * rows : (k + 1) * rows, :] = read(refs, spot, (0, rows)).astype(out.dtype)


def halve_kernel(spots, rows, bit, *refs):
    count = len(refs) - len(spots) - 2
    place, stays, send = refs[count], refs[count + 1 : -1], refs[-1]
    half = rows // 2
    mine = (place[0] // bit) % 2
    for k, spot in enumerate(spots):
        stays[k][...] = read(refs, spot, (pl.multiple_of(mine * half, half), half))
        leave = read(refs, spot, (pl.multiple_of((1 - mine) * half, half), half))
        send[k * half : (k + 1) * half, :] = leave.astype(BF)


def whole_kernel(spots, rows, *refs):
    keep, send = refs[-2:]
    value = read(refs, spots[0], (0, rows))
    keep[...] = value
    send[...] = value.astype(BF)


def join_kernel(bit, own, other, place, out):
    half = own.shape[0]
    mine = (place[0] // bit) % 2
    out[pl.ds(pl.multiple_of(mine * half, half), half), :] = own[...].astype(out.dtype)
    out[pl.ds(pl.multiple_of((1 - mine) * half, half), half), :] = other[...].astype(out.dtype)


def finish_kernel(bit, turned, own, other, place, *refs):
    outs, low = refs[:-1], refs[-1]
    join_kernel(bit, own, other, place, low)
    col = 0
    for out, turn in zip(outs, turned):
        span = out.shape[0] if turn else out.shape[1]
        part = low[:, col : col + span]
        out[...] = part.T if turn else part
        col += span


def vector_kernel(parts, *refs):
    out = refs[-1]
    out[...] = jnp.zeros_like(out)
    row = 0
    for ref, n in zip(refs, parts):
        out[row : row + n, : ref.shape[1]] = ref[:n, :]
        row += n


def vector_add_kernel(bit, heads, fixed, mine, got, out):
    out[:fixed, :] = mine[:fixed, :] + got[:fixed, :]
    for k in range(heads):
        other = fixed + (k ^ bit if bit < heads else k)
        out[fixed + k : fixed + k + 1, :] = (
            mine[fixed + k : fixed + k + 1, :] + got[other : other + 1, :]
        )


class Links:
    def __init__(self, mesh):
        self.dp, self.head = mesh.shape["dp"], mesh.shape["head"]

    def swap(self, value, bit):
        total = self.dp * self.head
        return lax.ppermute(value, AXES, [(i, i ^ bit) for i in range(total)])


class Chain:
    def __init__(self, links, kernels, place):
        self.links, self.kernels, self.place = links, kernels, place
        self.slots, self.bit = {}, 2

    def give(self, slot, value):
        self.rows, self.cols = value.shape
        if slot % 2:
            got = self.links.swap(value, 1)
            self.slots.setdefault(slot - 1, []).append((got, 0))
        else:
            self.slots.setdefault(slot, []).append((value, 0))

    def spots(self, sums):
        arrays, spots = [], []
        for terms in sums:
            spots.append([])
            for value, first in terms:
                known = [i for i, a in enumerate(arrays) if a is value]
                if not known:
                    arrays.append(value)
                    known = [len(arrays) - 1]
                spots[-1].append((known[0], first))
        return arrays, spots

    def head(self):
        leave = [k for k in self.slots if k & self.bit]
        arrays, spots = self.spots([self.slots[k] for k in leave])
        (send,) = self.kernels.call(
            functools.partial(send_kernel, spots, self.rows),
            [((len(leave) * self.rows, self.cols), BF)],
            *arrays,
            name="send",
        )
        got = self.links.swap(send, self.bit)
        for i, k in enumerate(leave):
            del self.slots[k]
            self.slots[k ^ self.bit].append((got, i * self.rows))
        self.bit *= 2

    def fold(self, slot):
        arrays, spots = self.spots([self.slots[slot]])
        (value,) = self.kernels.call(
            functools.partial(send_kernel, spots, self.rows),
            [((self.rows, self.cols), F32)],
            *arrays,
            name="fold",
        )
        self.slots[slot] = [(value, 0)]

    def halve(self, bit):
        keys = list(self.slots)
        arrays, spots = self.spots([self.slots[k] for k in keys])
        half = self.rows // 2
        got = self.kernels.call(
            functools.partial(halve_kernel, spots, self.rows, bit),
            [((half, self.cols), F32)] * len(keys) + [((len(keys) * half, self.cols), BF)],
            *arrays,
            self.place,
            scalars=1,
            name="halve",
        )
        came = self.links.swap(got[-1], bit * self.links.head)
        self.slots = {k: [(got[i], 0), (came, i * half)] for i, k in enumerate(keys)}
        self.rows = half

    def whole(self, bit):
        arrays, spots = self.spots([self.slots[0]])
        keep, send = self.kernels.call(
            functools.partial(whole_kernel, spots, self.rows),
            [((self.rows, self.cols), F32), ((self.rows, self.cols), BF)],
            *arrays,
            name="whole",
        )
        self.slots = {0: [(keep, 0), (self.links.swap(send, bit * self.links.head), 0)]}

    def settle(self, bit):
        arrays, spots = self.spots([self.slots[0]])
        (self.own,) = self.kernels.call(
            functools.partial(send_kernel, spots, self.rows),
            [((self.rows, self.cols), BF)],
            *arrays,
            name="settle",
        )
        self.got, self.last = self.links.swap(self.own, bit * self.links.head), bit

    def double(self, bit):
        self.rows *= 2
        (self.own,) = self.kernels.call(
            functools.partial(join_kernel, self.last),
            [((self.rows, self.cols), BF)],
            self.own,
            self.got,
            self.place,
            scalars=1,
            name="join",
        )
        self.got, self.last = self.links.swap(self.own, bit * self.links.head), bit

    def finish(self, outs, turned):
        return self.kernels.call(
            functools.partial(finish_kernel, self.last, turned),
            [(o, F32, True) for o in outs],
            self.own,
            self.got,
            self.place,
            scalars=1,
            scratch=[((2 * self.rows, self.cols), F32)],
            name="finish",
        )


def make(mesh):
    links = Links(mesh)
    nslots = links.head
    bits = [2**k for k in range(links.dp.bit_length() - 1)]

    def shards(
        residual_in,
        cotangent,
        triple_weight,
        proj_weight,
        up_weight,
        up_bias,
        down_weight,
        proj_bias,
        down_bias,
        first_gain,
        first_shift,
        second_gain,
        second_shift,
        start_steps,
        cond_counts,
        valid_lengths,
    ):
        kernels = Kernels()
        call = kernels.call
        rows, width = residual_in.shape
        seqs = rows // SEQ
        hidden = up_weight.shape[1]
        row = lambda v: v.reshape(1, -1)
        proj_bias, down_bias, first_gain, first_shift, second_gain, second_shift = map(
            row, (proj_bias, down_bias, first_gain, first_shift, second_gain, second_shift)
        )
        place = lax.axis_index("dp").astype(jnp.int32).reshape(1)
        base = (lax.axis_index("head") * seqs).astype(jnp.int32).reshape(1)
        scalars = (base, start_steps, cond_counts, valid_lengths)
        group = 2 * HEAD_DIM // proj_weight.shape[0]
        units = nslots // group
        (packed,) = call(
            pack_kernel,
            [((proj_weight.shape[0] + 16, width), BF)],
            proj_weight,
            row(up_bias),
            place,
            base,
            scalars=2,
            name="pack",
        )

        own = {"t": triple_weight, "p": packed, "u": up_weight, "d": down_weight}
        slots = {}
        for key, value in own.items():
            far = {0: value}
            bit = nslots // 2
            while bit > 1:
                far.update({k | bit: links.swap(v, bit) for k, v in list(far.items())})
                bit //= 2
            far[1] = links.swap(value, 1)
            slots[key] = far

        def relay(key, k):
            value = slots[key][k]
            (value,) = call(relay_kernel, [(value.shape, BF)], value, name="relay")
            slots[key][k + 1] = links.swap(value, 1)

        def unit_weight(key, u, axis):
            parts = [slots[key][k] for k in range(u * group, (u + 1) * group)]
            if group == 1:
                return parts[0]
            span = own[key].shape[axis] - (16 if key == "p" else 0)
            shape = (group * span, width) if axis == 0 else (width, group * span)
            body = functools.partial(pair_kernel, axis, span)
            return call(body, [(shape, BF)], *parts, name="pair")[0]

        first, first_t, out_low, out_t = call(
            prep_kernel,
            [((rows, width), BF), ((width, rows), BF)] * 2,
            residual_in,
            cotangent,
            first_gain,
            first_shift,
            name="prep",
        )
        triple_w, proj_w, triples, probs, mixeds = {}, {}, {}, {}, {}

        def attend_call(which):
            n = len(which)
            for u in which:
                triple_w[u] = unit_weight("t", u, 1)
            got = call(
                functools.partial(attend_kernel, n, seqs),
                [((rows, 6 * HEAD_DIM), BF)] * n
                + [((2 * seqs, SEQ, SEQ), F32)] * n
                + [((rows, 2 * HEAD_DIM), BF)] * n,
                first,
                *(triple_w[u] for u in which),
                *scalars,
                scalars=4,
                name="attend",
            )
            for i, u in enumerate(which):
                triples[u], probs[u], mixeds[u] = got[i], got[n + i], got[2 * n + i]

        early = list(range(max(1, 2 // group)))
        attend_call(early)
        for u in early:
            proj_w[u] = unit_weight("p", u, 0)
        (acc,) = call(
            functools.partial(project_kernel, len(early)),
            [((rows, width), F32)],
            *(mixeds[u] for u in early),
            *(proj_w[u] for u in early),
            name="project",
        )
        late = [u for u in range(units) if u not in early]
        for k in range(2, nslots, 2):
            relay("t", k)
            for u in sorted({k // group, (k + 1) // group}):
                attend_call([u])
                if u * group <= k:
                    relay("p", k)
        for u in late:
            proj_w[u] = unit_weight("p", u, 0)
        middle, second, second_t = call(
            functools.partial(second_kernel, len(late)),
            [((rows, width), F32), ((rows, width), BF), ((width, rows), BF)],
            *(mixeds[u] for u in late),
            *(proj_w[u] for u in late),
            acc,
            residual_in,
            proj_bias,
            second_gain,
            second_shift,
            name="second",
        )

        def kind(k):
            return BF if k % 2 else F32

        acts, slopes, biases = {}, {}, {}
        down_sum, up_sum, attn_sum = (Chain(links, kernels, place) for _ in range(3))

        def hidden_call(which):
            n = len(which)
            got = call(
                functools.partial(hidden_kernel, n),
                [((rows, hidden), BF)] * n
                + [((rows, hidden), F32)] * n
                + [((width, hidden), kind(k)) for k in which],
                second,
                out_t,
                *(slots["u"][k] for k in which),
                *(slots["p"][k] for k in which),
                name="hidden",
            )
            for i, k in enumerate(which):
                acts[k], slopes[k] = got[i], got[n + i]
                down_sum.give(k, got[2 * n + i])

        def hidden_back_call(which, *acc):
            n = len(which)
            got = call(
                functools.partial(hidden_back_kernel, n, not acc),
                [((width, hidden), kind(k)) for k in which]
                + [((1, hidden), F32)] * n
                + [((rows, width), F32)],
                out_low,
                second_t,
                *(slots["u"][k] for k in which),
                *(slots["d"][k] for k in which),
                *(slopes[k] for k in which),
                *acc,
                scratch=[((rows, hidden), BF)] * n,
                name="hidden_back",
            )
            for i, k in enumerate(which):
                up_sum.give(k, got[i])
                biases[k] = got[n + i]
            return got[2 * n]

        hidden_call([0, 1])
        acc = hidden_back_call([0, 1])
        for k in range(2, nslots, 2):
            relay("u", k)
            hidden_call([k])
            if k == 2:
                down_sum.fold(0)
            hidden_call([k + 1])
            if k == 2:
                up_sum.fold(0)
        for k in range(2, nslots, 2):
            relay("d", k)
            acc = hidden_back_call([k], acc)
            if k == 2:
                down_sum.head()
            acc = hidden_back_call([k + 1], acc)
        grad_middle, middle_low, middle_t, sums_middle = call(
            middle_kernel,
            [((rows, width), F32), ((rows, width), BF), ((width, rows), BF), ((8, width), F32)],
            acc,
            middle,
            second_gain,
            cotangent,
            name="middle",
        )
        up_sum.head()
        while up_sum.bit < nslots:
            down_sum.head()
            up_sum.head()

        attn_width = 8 * HEAD_DIM // group
        gtls = {}

        def attend_back_call(which):
            n = len(which)
            got = call(
                functools.partial(attend_back_kernel, n, group, seqs),
                [((rows, 6 * HEAD_DIM), BF)] * n
                + [((width, attn_width), kind(k)) for u in which for k in range(group * u, group * u + group)],
                middle_low,
                middle_t,
                first_t,
                *(proj_w[u] for u in which),
                *(triples[u] for u in which),
                *(probs[u] for u in which),
                *(mixeds[u] for u in which),
                scratch=[((rows, 2 * HEAD_DIM), BF)] * n,
                name="attend_back",
            )
            for i, u in enumerate(which):
                gtls[u] = got[i]
                for j in range(group):
                    attn_sum.give(u * group + j, got[n + i * group + j])

        attend_back_call(late[::-1])
        down_sum.halve(bits[0])
        attend_back_call(early[::-1])
        attn_sum.head()
        while attn_sum.bit < nslots:
            attn_sum.head()
        grad_input, sums_input = call(
            functools.partial(input_kernel, units),
            [((rows, width), F32, True), ((8, width), F32)],
            *(gtls[u] for u in range(units)),
            *(triple_w[u] for u in range(units)),
            residual_in,
            first_gain,
            grad_middle,
            cotangent,
            name="input",
        )
        (vector,) = call(
            functools.partial(vector_kernel, [3, 3] + [1] * nslots),
            [((16, width), F32)],
            sums_middle,
            sums_input,
            *(biases[k] for k in range(nslots)),
            name="vector",
        )
        vector_bits = [2**k for k in range((links.dp * links.head).bit_length() - 1)]
        vector_got = links.swap(vector, vector_bits[0])

        def vector_step():
            nonlocal vector, vector_got
            bit = vector_bits.pop(0)
            (vector,) = call(
                functools.partial(vector_add_kernel, bit, nslots, 6),
                [((16, width), F32)],
                vector,
                vector_got,
                name="vector_add",
            )
            if vector_bits:
                vector_got = links.swap(vector, vector_bits[0])

        up_sum.halve(bits[0])
        down_sum.halve(bits[1])
        for bit in bits[2:-1]:
            down_sum.halve(bit)
        (block_out,) = call(
            functools.partial(output_kernel, nslots),
            [((rows, width), F32, True)],
            *(acts[k] for k in range(nslots)),
            *(slots["d"][k] for k in range(nslots)),
            middle,
            down_bias,
            name="output",
        )
        vector_step()
        up_sum.halve(bits[1])
        for bit in bits[2:-1]:
            up_sum.halve(bit)
        down_sum.whole(bits[-1])
        attn_sum.halve(bits[0])
        vector_step()
        up_sum.whole(bits[-1])
        down_sum.settle(bits[-2])
        for bit in bits[1:-1]:
            attn_sum.halve(bit)
        vector_step()
        up_sum.settle(bits[-2])
        back = bits[-3::-1]
        for bit in back:
            down_sum.double(bit)
        attn_sum.whole(bits[-1])
        vector_step()
        for bit in back:
            up_sum.double(bit)
        attn_sum.settle(bits[-2])
        while vector_bits:
            vector_step()
        (grad_down,) = down_sum.finish([(hidden, width)], [True])
        (grad_up,) = up_sum.finish([(width, hidden)], [False])
        for bit in back:
            attn_sum.double(bit)
        grad_triple, grad_proj = attn_sum.finish(
            [(width, 3 * attn_width // 4), (attn_width // 4, width)], [False, True]
        )
        return (
            block_out,
            grad_input,
            grad_triple,
            grad_proj,
            grad_up,
            vector[6, :hidden],
            grad_down,
            vector[0],
            vector[3],
            vector[4],
            vector[5],
            vector[1],
            vector[2],
        )

    return shards


def solution(mesh):
    in_specs = (
        P(("dp", "head"), None),
        P(("dp", "head"), None),
        P(None, "head"),
        P("head", None),
        P(None, "head"),
        P("head"),
        P("head", None),
        P(),
        P(),
        P(),
        P(),
        P(),
        P(),
        P("dp"),
        P("dp"),
        P("dp"),
    )
    out_specs = (
        P(("dp", "head"), None),
        P(("dp", "head"), None),
        P(None, "head"),
        P("head", None),
        P(None, "head"),
        P("head"),
        P("head", None),
        P(),
        P(),
        P(),
        P(),
        P(),
        P(),
    )
    return jax.shard_map(
        make(mesh), mesh=mesh, in_specs=in_specs, out_specs=out_specs, check_vma=False
    )
```

```python
import functools
import types

import jax
import jax.numpy as jnp
from jax import lax
from jax.experimental import pallas as pl
from jax.experimental.pallas import tpu as pltpu
from jax.sharding import PartitionSpec as P

HEAD_DIM = 64
SEQ = 128
EPSILON = 1e-05
NEG_FILL = -1e30
BF = jnp.bfloat16
F32 = jnp.float32
AXES = ("dp", "head")
CHUNK = 128
VMEM_LIMIT = 8 * 2**20


def nn(a, b):
    return lax.dot_general(a, b, (((1,), (0,)), ((), ())), preferred_element_type=F32)


def nt(a, b):
    return lax.dot_general(a, b, (((1,), (1,)), ((), ())), preferred_element_type=F32)


def tn(a, b):
    return lax.dot_general(a, b, (((0,), (0,)), ((), ())), preferred_element_type=F32)


class Kernels:
    def __init__(self):
        self.token = jnp.zeros((8, 128), F32)

    def call(self, body, outs, *args, scalars=0, scratch=(), also=(), name=None):
        vmem = pl.BlockSpec(memory_space=pltpu.VMEM)
        smem = pl.BlockSpec(memory_space=pltpu.SMEM)
        plain, count = len(args) - scalars, len(args)

        mine = count + len(also)
        last = mine + 1 + len(outs)

        def ordered(*refs):
            refs[last][...] = refs[mine][...]
            body(*refs[:count], *refs[mine + 1 : last], *refs[last + 1 :])

        got = pl.pallas_call(
            ordered,
            out_shape=[jax.ShapeDtypeStruct(*out[:2]) for out in outs]
            + [jax.ShapeDtypeStruct((8, 128), F32)],
            in_specs=[vmem] * plain + [smem] * scalars + [vmem] * (len(also) + 1),
            out_specs=[vmem] * (len(outs) + 1),
            compiler_params=pltpu.CompilerParams(vmem_limit_bytes=VMEM_LIMIT),
            scratch_shapes=[pltpu.VMEM(*s) for s in scratch],
            cost_estimate=pl.CostEstimate(flops=0, bytes_accessed=0, transcendentals=0),
            name=name,
        )(*args, *also, self.token)
        self.token = got[-1]
        return got[:-1]

    def wait(self, *arrays):
        self.call(touch_kernel, [], *arrays, name="touch")


def centred(rows):
    centre = rows - jnp.mean(rows, axis=-1, keepdims=True)
    spread = jnp.mean(centre * centre, axis=-1, keepdims=True)
    rstd = lax.rsqrt(spread + EPSILON)
    return centre * rstd, rstd


def norm_back(grad, rows, gain):
    xhat, rstd = centred(rows)
    q = grad * gain
    inner = jnp.mean(q * xhat, axis=-1, keepdims=True)
    row = rstd * (q - jnp.mean(q, axis=-1, keepdims=True) - xhat * inner)
    return row, jnp.sum(grad * xhat, axis=0, keepdims=True), jnp.sum(grad, axis=0, keepdims=True)


def prep_kernel(res, gain, shift, first, first_t):
    for r in range(0, res.shape[0], CHUNK):
        xhat, _ = centred(res[r : r + CHUNK, :])
        low = (xhat * gain[...] + shift[...]).astype(BF)
        first[r : r + CHUNK, :] = low
        first_t[:, r : r + CHUNK] = low.T


def out_kernel(cot, out_low, out_t):
    for r in range(0, cot.shape[0], CHUNK):
        low = cot[r : r + CHUNK, :].astype(BF)
        out_low[r : r + CHUNK, :] = low
        out_t[:, r : r + CHUNK] = low.T


def lanes_low(shape):
    return lax.broadcasted_iota(jnp.int32, shape, 1) < HEAD_DIM


def half_turn(block):
    return jnp.concatenate([block[:, HEAD_DIM:], block[:, :HEAD_DIM]], 1)


def mask_of(start, count, length):
    m = lax.broadcasted_iota(jnp.int32, (SEQ, SEQ), 0)
    n = lax.broadcasted_iota(jnp.int32, (SEQ, SEQ), 1)
    group_m = jnp.maximum((m * 43) >> 8, start)
    group_n = jnp.maximum((n * 43) >> 8, start)
    seen = (m < length) & ((group_m <= group_n) | (m < count))
    return jnp.where(seen, 0.0, NEG_FILL)


def blocks_of(triple, s):
    at = slice(s * SEQ, (s + 1) * SEQ)
    b0, b1, b2 = (triple[at, c * 128 : (c + 1) * 128] for c in range(3))
    low, zero = lanes_low(b0.shape), jnp.zeros(b0.shape, BF)
    keys = jnp.concatenate([jnp.where(low, zero, b0), jnp.where(low, b2, zero)], 0)
    values = jnp.concatenate([jnp.where(low, b1, zero), jnp.where(low, zero, b2)], 0)
    queries = half_turn(jnp.where(low, b0, b1)) * jnp.asarray(HEAD_DIM**-0.5, BF)
    return keys, values, queries


def attend(first, weight, triple, probs, mixed, scalars, seqs):
    triple[...] = nn(first[...], weight[...]).astype(BF)
    base, starts, counts, lengths = scalars
    parts = [blocks_of(triple, s) for s in range(seqs)]
    for s, (keys, _, queries) in enumerate(parts):
        probs[s] = nt(keys, queries)
    for s in range(seqs):
        bias = mask_of(*(ref[base + s] for ref in (starts, counts, lengths)))
        for h in range(2):
            at = slice(h * SEQ, (h + 1) * SEQ)
            score = probs[s, at, :] + bias
            weights = jnp.exp(score - jnp.max(score, axis=0, keepdims=True))
            probs[s, at, :] = weights * (1.0 / jnp.sum(weights, axis=0, keepdims=True))
    for s, (_, values, _) in enumerate(parts):
        mixed[s * SEQ : (s + 1) * SEQ, :] = tn(probs[s].astype(BF), values).astype(BF)


def attend_back(middle_low, proj, triple, probs, seqs, gtl, grad_mixed, grad_probs):
    grad_mixed[...] = nn(middle_low[...], proj[: middle_low.shape[1], :]).astype(BF)
    parts = [blocks_of(triple, s) for s in range(seqs)]
    spots = [slice(s * SEQ, (s + 1) * SEQ) for s in range(seqs)]
    for s, (_, values, _) in enumerate(parts):
        grad_probs[s] = nt(values, grad_mixed[spots[s], :])
    lows = []
    for s in range(seqs):
        scores = []
        for h in range(2):
            at = slice(h * SEQ, (h + 1) * SEQ)
            prob, grad = probs[s, at, :], grad_probs[s, at, :]
            inner = jnp.sum(grad * prob, axis=0, keepdims=True)
            scores.append((prob * (grad - inner)).astype(BF))
        lows.append(jnp.concatenate(scores, 0))
    low = lanes_low((SEQ, 2 * HEAD_DIM))
    for s, (keys, _, queries) in enumerate(parts):
        grad_queries = half_turn(tn(lows[s], keys) * HEAD_DIM**-0.5)
        grad_keys = nn(lows[s], queries)
        grad_values = nn(probs[s].astype(BF), grad_mixed[spots[s], :])
        gtl[spots[s], 0:128] = jnp.where(low, grad_queries, grad_keys[:SEQ]).astype(BF)
        gtl[spots[s], 128:256] = jnp.where(low, grad_values[:SEQ], grad_queries).astype(BF)
        gtl[spots[s], 256:384] = jnp.where(low, grad_keys[SEQ:], grad_values[SEQ:]).astype(BF)


def gelu_parts(x):
    c0, c1 = 0.7978845608028654, 0.044715
    square = x * x
    t = jnp.tanh(x * (c0 + (c0 * c1) * square))
    h = 0.5 * (1.0 + t)
    slope = h + (0.5 * x) * (1.0 - t * t) * (c0 + (3.0 * c0 * c1) * square)
    return x * h, slope


def pack_kernel(proj, bias, place, base, out, *more):
    deep, span = proj.shape[1], out.shape[1]
    out[:deep, :] = proj[...].T
    rows = bias.shape[1] // span
    out[deep:, :] = jnp.concatenate(
        [bias[:, k * span : (k + 1) * span] for k in range(rows)]
        + [jnp.zeros((16 - rows, span), out.dtype)],
        0,
    )


def bundle_kernel(proj, bias, down, place, base, out, bundle):
    pack_kernel(proj, bias, place, base, out)
    deep, span = out.shape
    bundle[:deep, :] = out[...]
    half, per = down.shape[0] // 2, down.shape[1] // span
    rows = down[pl.ds(pl.multiple_of((place[0] % 2) * half, half), half), :]
    for k in range(per):
        bundle[deep + k * half : deep + (k + 1) * half, :] = rows[:, k * span : (k + 1) * span]


def unbundle_kernel(bundle, out, rows):
    deep, span = out.shape
    out[...] = bundle[:deep, :]
    half = rows.shape[0]
    for k in range(rows.shape[1] // span):
        rows[:, k * span : (k + 1) * span] = bundle[deep + k * half : deep + (k + 1) * half, :]


def pair_kernel(*refs):
    out, col = refs[-1], 0
    for part in refs[:-1]:
        out[:, col : col + part.shape[1]] = part[...]
        col += part.shape[1]


def touch_kernel(*refs):
    pass


def relay_kernel(value, out):
    out[...] = value[...]


def attend_kernel(units, seqs, *refs):
    refs = list(refs)
    take = lambda n: [refs.pop(0) for _ in range(n)]
    (first,) = take(1)
    weights = take(units)
    scalars = take(4)
    scalars = [scalars[0][0]] + scalars[1:]
    triples, probs, mixeds = take(units), take(units), take(units)
    for u in range(units):
        attend(first, weights[u], triples[u], probs[u], mixeds[u], scalars, seqs)


def project_kernel(units, *refs):
    mixeds, projs, acc = refs[:units], refs[units : 2 * units], refs[2 * units]
    acc[...] = sum(
        nt(mixeds[u][...], projs[u][: acc.shape[1], :]) for u in range(units)
    )


def second_kernel(units, *refs):
    refs = list(refs)
    take = lambda n: [refs.pop(0) for _ in range(n)]
    mixeds, projs = take(units), take(units)
    acc, residual, bias, gain, shift, middle, second, second_t = refs
    for r in range(0, acc.shape[0], CHUNK):
        at = slice(r, r + CHUNK)
        out = acc[at, :] + sum(
            nt(mixeds[u][at, :], projs[u][: acc.shape[1], :]) for u in range(units)
        )
        out = residual[at, :] + out + bias[...]
        middle[at, :] = out
        xhat, _ = centred(out)
        low = (xhat * gain[...] + shift[...]).astype(BF)
        second[at, :] = low
        second_t[:, at] = low.T


def hidden_kernel(slots, *refs):
    refs = list(refs)
    take = lambda n: [refs.pop(0) for _ in range(n)]
    second, out_t = take(2)
    ups, biases = take(slots), take(slots)
    acts, slopes, grads = take(slots), take(slots), take(slots)
    for j in range(slots):
        span, deep = biases[j].shape[1], second.shape[1]
        bias = jnp.concatenate(
            [biases[j][deep + k : deep + k + 1, :] for k in range(ups[j].shape[1] // span)], 1
        ).astype(F32)
        for r in range(0, second.shape[0], 2 * CHUNK):
            at = slice(r, r + 2 * CHUNK)
            act, slope = gelu_parts(nn(second[at, :], ups[j][...]) + bias)
            acts[j][at, :] = act.astype(BF)
            slopes[j][at, :] = slope
        grads[j][...] = nn(out_t[...], acts[j][...]).astype(grads[j].dtype)


def hidden_back_kernel(pieces, first_call, *refs):
    refs, slots = list(refs), len(pieces)
    take = lambda n: [refs.pop(0) for _ in range(n)]
    out_low, second_t = take(2)
    ups, downs, slopes = take(slots), take(slots), take(slots)
    acc_in = None if first_call else take(1)[0]
    grads, biases = [take(n) for n in pieces], take(slots)
    (acc,) = take(1)
    pre = take(slots)
    for j in range(slots):
        total = 0.0
        for r in range(0, out_low.shape[0], 2 * CHUNK):
            at = slice(r, r + 2 * CHUNK)
            low = (nt(out_low[at, :], downs[j][...]) * slopes[j][at, :]).astype(BF)
            pre[j][at, :] = low
            total = total + jnp.sum(low.astype(F32), axis=0, keepdims=True)
        biases[j][...] = total
        grad, first = nn(second_t[...], pre[j][...]), 0
        for out in grads[j]:
            out[...] = grad[first : first + out.shape[0], :].astype(out.dtype)
            first += out.shape[0]
    for r in range(0, out_low.shape[0], 2 * CHUNK):
        at = slice(r, r + 2 * CHUNK)
        out = sum(nt(pre[j][at, :], ups[j][...]) for j in range(slots))
        acc[at, :] = out if first_call else acc_in[at, :] + out


def middle_kernel(grad_second, middle, gain, cot, grad_middle, middle_low, middle_t, sums):
    totals = [0.0, 0.0, 0.0]
    for r in range(0, cot.shape[0], CHUNK):
        at = slice(r, r + CHUNK)
        row, dgain, dshift = norm_back(grad_second[at, :], middle[at, :], gain[...])
        grad = cot[at, :] + row
        grad_middle[at, :] = grad
        low = grad.astype(BF)
        middle_low[at, :] = low
        middle_t[:, at] = low.T
        parts = (jnp.sum(grad, axis=0, keepdims=True), dgain, dshift)
        totals = [t + p for t, p in zip(totals, parts)]
    for i, t in enumerate(totals):
        sums[i : i + 1, :] = t


def attend_back_kernel(units, group, pieces, seqs, *refs):
    refs = list(refs)
    take = lambda n: [refs.pop(0) for _ in range(n)]
    middle_low, middle_t, first_t = take(3)
    projs, triples, probs, mixeds = take(units), take(units), take(units), take(units)
    gtls, grads = take(units), [take(n) for n in pieces]
    grad_mixed, grad_probs = take(units), take(units)
    span, small = 6 * HEAD_DIM // group, 2 * HEAD_DIM // group
    for u in range(units):
        attend_back(
            middle_low,
            projs[u],
            triples[u],
            probs[u],
            seqs,
            gtls[u],
            grad_mixed[u],
            grad_probs[u],
        )
        grad = nn(first_t[...], gtls[u][...])
        proj_grad = nn(middle_t[...], mixeds[u][...])
        for k in range(group):
            first = 0
            for out in grads[u * group + k]:
                at = slice(first, first + out.shape[0])
                first += out.shape[0]
                out[:, :span] = grad[at, k * span : (k + 1) * span].astype(out.dtype)
                out[:, span:] = proj_grad[at, k * small : (k + 1) * small].astype(out.dtype)


def input_kernel(units, *refs):
    refs = list(refs)
    take = lambda n: [refs.pop(0) for _ in range(n)]
    gtls, weights = take(units), take(units)
    residual, gain, grad_middle, cot = take(4)
    grad_input, sums = take(2)
    totals = [0.0, 0.0, 0.0]
    for r in range(0, cot.shape[0], CHUNK):
        at = slice(r, r + CHUNK)
        grad = sum(nt(gtls[u][at, :], weights[u][...]) for u in range(units))
        row, dgain, dshift = norm_back(grad, residual[at, :], gain[...])
        grad_input[at, :] = grad_middle[at, :] + row
        parts = (jnp.sum(cot[at, :], axis=0, keepdims=True), dgain, dshift)
        totals = [t + p for t, p in zip(totals, parts)]
    for i, t in enumerate(totals):
        sums[i : i + 1, :] = t


def output_kernel(slots, *refs):
    acts, downs = refs[:slots], refs[slots : 2 * slots]
    middle, bias, out = refs[2 * slots :]
    for r in range(0, middle.shape[0], 2 * CHUNK):
        at = slice(r, r + 2 * CHUNK)
        total = sum(nn(acts[j][at, :], downs[j][...]) for j in range(slots))
        out[at, :] = middle[at, :] + total + bias[...]


def total(terms):
    out = terms[0]
    for term in terms[1:]:
        out = out + term
    return out


def read(refs, spots, at):
    terms = []
    for where, first in spots:
        if len(where) > 1:
            terms.append(jnp.concatenate([refs[i][...] for i in where], 0).astype(F32))
        else:
            terms.append(refs[where[0]][pl.ds(first + at[0], at[1]), :].astype(F32))
    return total(terms)


def rider_rows(rider, cols):
    return 2 * rider[0] * -(-(rider[1] // 128) // max(1, cols // 128))


def pack_rider(rider, out, first):
    per, deep = max(1, out.shape[1] // 128), 2 * rider.shape[0]
    high = rider.astype(BF)
    rest = (rider - high.astype(F32)).astype(BF)
    for j in range(rider.shape[1] // 128):
        at, row, col = slice(j * 128, (j + 1) * 128), first + deep * (j // per), 128 * (j % per)
        block = jnp.concatenate([high[:, at], rest[:, at]], 0)
        out[row : row + deep, col : col + 128] = block


def unpack_rider(value, first, shape):
    rows, per, parts = shape[0], max(1, value.shape[1] // 128), []
    for j in range(shape[1] // 128):
        row, col = first + 2 * rows * (j // per), 128 * (j % per)
        block = value[row : row + 2 * rows, col : col + 128].astype(F32)
        parts.append(block[:rows, :] + block[rows:, :])
    return jnp.concatenate(parts, 1)


def rider_total(refs, ride):
    kept, came, first = ride
    rider = refs[kept][...]
    for i in came:
        rider = rider + unpack_rider(refs[i], first, rider.shape)
    return rider


def send_kernel(spots, rows, *refs):
    count = 1 + max(i for spot in spots for where, _ in spot for i in where)
    outs = refs[count:]
    if len(outs) > 1:
        value = read(refs, spots[0], (0, rows)).astype(BF)
        for k, out in enumerate(outs):
            out[...] = value[k * out.shape[0] : (k + 1) * out.shape[0], :]
        return
    (out,) = outs
    used = len(spots) * rows
    for k, spot in enumerate(spots):
        out[k * rows : (k + 1) * rows, :] = read(refs, spot, (0, rows)).astype(out.dtype)
    if used < out.shape[0]:
        out[used:, :] = jnp.zeros((out.shape[0] - used, out.shape[1]), out.dtype)


def halve_kernel(spots, rows, bit, ride, *refs):
    refs = list(refs)
    if ride:
        rider_keep = refs.pop()
    send = refs.pop()
    stays = [refs.pop() for _ in spots][::-1]
    place = refs.pop()
    half = rows // 2
    mine = (place[0] // bit) % 2
    for k, spot in enumerate(spots):
        stays[k][...] = read(refs, spot, (pl.multiple_of(mine * half, half), half))
        leave = read(refs, spot, (pl.multiple_of((1 - mine) * half, half), half))
        send[k * half : (k + 1) * half, :] = leave.astype(BF)
    room = len(spots) * half
    if room < send.shape[0]:
        send[room:, :] = jnp.zeros((send.shape[0] - room, send.shape[1]), BF)
    if ride:
        rider = rider_total(refs, ride)
        rider_keep[...] = rider
        pack_rider(rider, send, len(spots) * half)


def whole_kernel(spots, rows, ride, *refs):
    refs = list(refs)
    if ride:
        rider_keep = refs.pop()
    send, keep = refs.pop(), refs.pop()
    value = read(refs, spots[0], (0, rows))
    keep[...] = value
    send[:rows, :] = value.astype(BF)
    send[rows:, :] = jnp.zeros((send.shape[0] - rows, send.shape[1]), BF)
    if ride:
        rider = rider_total(refs, ride)
        rider_keep[...] = rider
        pack_rider(rider, send, rows)


def settle_kernel(spots, rows, ride, *refs):
    refs = list(refs)
    if ride:
        rider_out = refs.pop()
    out = refs.pop()
    out[...] = read(refs, spots[0], (0, rows)).astype(out.dtype)
    if ride:
        rider_out[...] = rider_total(refs, ride)


def join_kernel(bit, own, other, place, out):
    half = own.shape[0]
    mine = (place[0] // bit) % 2
    out[pl.ds(pl.multiple_of(mine * half, half), half), :] = own[...].astype(out.dtype)
    out[pl.ds(pl.multiple_of((1 - mine) * half, half), half), :] = other[...].astype(out.dtype)


def finish_kernel(bit, blocks, turned, own, other, place, *refs):
    outs, low = refs[:-1], refs[-1]
    join_kernel(bit, own, other, place, low)
    rows, col = low.shape[0] // len(blocks), 0
    for out, turn in zip(outs, turned):
        span = out.shape[0] if turn else out.shape[1]
        for to, at in enumerate(blocks):
            part = low[at * rows : (at + 1) * rows, col : col + span]
            if turn:
                out[:, to * rows : (to + 1) * rows] = part.T
            else:
                out[to * rows : (to + 1) * rows, :] = part
        col += span


def vector_kernel(parts, *refs):
    out = refs[-1]
    out[...] = jnp.zeros_like(out)
    row = 0
    for ref, n in zip(refs, parts):
        out[row : row + n, : ref.shape[1]] = ref[:n, :]
        row += n


def vector_core_kernel(heads, fixed, mine, got, out):
    out[...] = jnp.zeros_like(out)
    out[:fixed, :] = mine[:fixed, :] + got[:fixed, :]
    for k in range(0, heads, 2):
        at, other, to = fixed + k, fixed + k + 1, fixed + k // 2
        out[to : to + 1, :] = mine[at : at + 1, :] + got[other : other + 1, :]


def vector_add_kernel(bit, fixed, mine, got, out):
    out[...] = mine[...] + got[...]
    for k in range(out.shape[0] - fixed):
        if k ^ bit < out.shape[0] - fixed:
            at, other = fixed + k, fixed + (k ^ bit)
            out[at : at + 1, :] = mine[at : at + 1, :] + got[other : other + 1, :]


def vector_last_kernel(bit, fixed, mine, got, *outs):
    for k in range(fixed + 1):
        other, span = (k if k < fixed else fixed + bit), outs[k].shape[1]
        outs[k][...] = mine[k : k + 1, :span] + got[other : other + 1, :span]


class Links:
    def __init__(self, mesh):
        self.dp, self.head = mesh.shape["dp"], mesh.shape["head"]

    def swap(self, value, bit):
        total = self.dp * self.head
        return lax.ppermute(value, AXES, [(i, i ^ bit) for i in range(total)])


class Chain:
    def __init__(self, links, kernels, place, room, tag):
        self.tag = tag
        self.room = room
        self.links, self.kernels, self.place = links, kernels, place
        self.slots, self.bit, self.halved = {}, 2, []
        self.rider, self.rider_came = None, []
        self.rider_first = 0

    def give(self, slot, *values):
        self.rows, self.cols = sum(v.shape[0] for v in values), values[0].shape[1]
        if slot % 2:
            got = [self.links.swap(v, 1) for v in values]
            self.slots.setdefault(slot - 1, []).insert(0, (got, 0))
        else:
            self.slots.setdefault(slot, []).insert(0, (list(values), 0))

    def give_later(self, slot, value):
        (value,) = self.kernels.call(relay_kernel, [(value.shape, BF)], value, name="relay")
        self.give(slot, value)

    def spots(self, sums):
        arrays, spots = [], []
        for terms in sums:
            spots.append([])
            for values, first in terms:
                where = []
                for value in values:
                    known = [i for i, a in enumerate(arrays) if a is value]
                    if not known:
                        arrays.append(value)
                        known = [len(arrays) - 1]
                    where.append(known[0])
                spots[-1].append((where, first))
        return arrays, spots

    def head(self, pieces=1, spare=False):
        leave = [k for k in self.slots if k & self.bit]
        arrays, spots = self.spots([self.slots[k] for k in leave])
        room = rider_rows(self.room, self.cols) if self.halved or spare else 0
        deep = len(leave) * self.rows + room
        sends = self.kernels.call(
            functools.partial(send_kernel, spots, self.rows),
            [((deep // pieces, self.cols), BF)] * pieces,
            *arrays,
            name="send_" + self.tag,
        )
        got = [self.links.swap(send, self.bit) for send in sends]
        for i, k in enumerate(leave):
            del self.slots[k]
            self.slots.setdefault(k ^ self.bit, []).append((got, i * self.rows))
        self.bit *= 2

    def fold(self, slot, count=2):
        arrays, spots = self.spots([self.slots[slot][:count]])
        (value,) = self.kernels.call(
            functools.partial(send_kernel, spots, self.rows),
            [((self.rows, self.cols), F32)],
            *arrays,
            name="fold_" + self.tag,
        )
        self.slots[slot][:count] = [([value], 0)]

    def ride(self, arrays):
        if self.rider is None:
            return None
        arrays.append(self.rider)
        came = [i for i, a in enumerate(arrays) if any(a is b for b in self.rider_came)]
        return len(arrays) - 1, came, self.rider_first

    def rode(self, kept, came, first):
        if self.rider is not None:
            self.rider, self.rider_came, self.rider_first = kept, came, first

    def halve(self, bit):
        keys = list(self.slots)
        arrays, spots = self.spots([self.slots[k] for k in keys])
        half = self.rows // 2
        ride = self.ride(arrays)
        rider = [(self.rider.shape, F32)] if ride else []
        more = rider_rows(self.room, self.cols) if self.halved or len(keys) == 1 else 0
        got = self.kernels.call(
            functools.partial(halve_kernel, spots, self.rows, bit, ride),
            [((half, self.cols), F32)] * len(keys)
            + [((len(keys) * half + more, self.cols), BF)]
            + rider,
            *arrays,
            self.place,
            scalars=1,
            name="halve_" + self.tag,
        )
        came = self.links.swap(got[len(keys)], bit * self.links.head)
        self.slots = {k: [([got[i]], 0), ([came], i * half)] for i, k in enumerate(keys)}
        self.rode(got[-1], [came], len(keys) * half)
        self.rows = half
        self.halved.append(bit)

    def whole(self, bit):
        arrays, spots = self.spots([self.slots[0]])
        ride = self.ride(arrays)
        rider = [(self.rider.shape, F32)] if ride else []
        more = rider_rows(self.room, self.cols)
        got = self.kernels.call(
            functools.partial(whole_kernel, spots, self.rows, ride),
            [((self.rows, self.cols), F32), ((self.rows + more, self.cols), BF)] + rider,
            *arrays,
            name="whole_" + self.tag,
        )
        came = self.links.swap(got[1], bit * self.links.head)
        self.slots = {0: [([got[0]], 0), ([came], 0)]}
        self.rode(got[-1], [came], self.rows)

    def settle(self, order):
        arrays, spots = self.spots([self.slots[0]])
        ride = self.ride(arrays)
        got = self.kernels.call(
            functools.partial(settle_kernel, spots, self.rows, ride),
            [((self.rows, self.cols), BF)] + ([(self.rider.shape, F32)] if ride else []),
            *arrays,
            name="settle_" + self.tag,
        )
        self.own, self.order, self.left = got[0], list(order), list(order)
        self.back()
        return got[-1]

    def back(self):
        self.last = self.left.pop(0)
        self.got = self.links.swap(self.own, self.last * self.links.head)

    def double(self):
        self.rows *= 2
        (self.own,) = self.kernels.call(
            functools.partial(join_kernel, self.last),
            [((self.rows, self.cols), BF)],
            self.own,
            self.got,
            self.place,
            scalars=1,
            name="join_" + self.tag,
        )
        self.back()

    def finish(self, outs, turned):
        blocks = []
        for to in range(2 ** len(self.order)):
            digits = {b: to >> (len(self.halved) - 1 - i) & 1 for i, b in enumerate(self.halved)}
            blocks.append(sum(digits[b] << i for i, b in enumerate(self.order)))
        if blocks == sorted(blocks):
            blocks = [0]
        return self.kernels.call(
            functools.partial(finish_kernel, self.last, blocks, turned),
            [(o, F32, True) for o in outs],
            self.own,
            self.got,
            self.place,
            scalars=1,
            scratch=[((2 * self.rows, self.cols), F32)],
            name="finish_" + self.tag,
        )


def make(mesh):
    links = Links(mesh)
    nslots = links.head
    bits = [2**k for k in range(links.dp.bit_length() - 1)]

    def shards(
        residual_in,
        cotangent,
        triple_weight,
        proj_weight,
        up_weight,
        up_bias,
        down_weight,
        proj_bias,
        down_bias,
        first_gain,
        first_shift,
        second_gain,
        second_shift,
        start_steps,
        cond_counts,
        valid_lengths,
    ):
        kernels = Kernels()
        call = kernels.call
        rows, width = residual_in.shape
        seqs = rows // SEQ
        hidden, proj_rows = up_weight.shape[1], proj_weight.shape[0]
        row = lambda v: v.reshape(1, -1)
        proj_bias, down_bias, first_gain, first_shift, second_gain, second_shift = map(
            row, (proj_bias, down_bias, first_gain, first_shift, second_gain, second_shift)
        )
        place = lax.axis_index("dp").astype(jnp.int32).reshape(1)
        base = (lax.axis_index("head") * seqs).astype(jnp.int32).reshape(1)
        scalars = (base, start_steps, cond_counts, valid_lengths)
        group = 2 * HEAD_DIM // proj_rows
        units = nslots // group

        slots = {}

        def far(key, value):
            known = {0: value}
            bit = nslots // 2
            while bit > 1:
                known.update({k | bit: links.swap(v, bit) for k, v in list(known.items())})
                bit //= 2
            slots[key] = known

        def near(key):
            slots[key][1] = links.swap(slots[key][0], 1)

        def relay(key, k):
            value = slots[key][k]
            (value,) = call(relay_kernel, [(value.shape, BF)], value, name="relay")
            slots[key][k + 1] = links.swap(value, 1)

        far("t", triple_weight)
        near("t")
        far("u", up_weight)
        near("u")
        slots["d"] = {0: down_weight, 1: links.swap(down_weight, 1)}
        shared = nslots == 4 and len(bits) > 1
        pack_shape = (width + 16, proj_rows)
        half = (down_weight.shape[0] // 2, width)
        evens, odds = range(2, nslots, 2), range(3, nslots, 2)
        early = list(range(max(1, 2 // group)))
        late = [u for u in range(units) if u not in early]
        triple_w, proj_w, triples, probs, mixeds = {}, {}, {}, {}, {}
        acts, slopes, biases, down_grads, up_grads = {}, {}, {}, {}, {}
        gtls, triple_grads = {}, {}
        room = (8 * -(-(6 + nslots // 2) // 8), width)
        down_sum, up_sum, triple_sum = (Chain(links, kernels, place, room, t) for t in "dut")
        middle_bits, there = bits[1:-1], bits[:-1]
        s = types.SimpleNamespace()
        thirds = [width // 48 * 16 + 16] * 2
        thirds = thirds + [width - sum(thirds)]

        def kind(k):
            return BF if k % 2 else F32

        def bundle():
            if shared:
                deep = pack_shape[0] + half[0] * width // proj_rows
                packed, sent = call(
                    bundle_kernel,
                    [(pack_shape, BF), ((deep, proj_rows), BF)],
                    proj_weight,
                    row(up_bias),
                    down_weight,
                    place,
                    base,
                    scalars=2,
                    name="bundle",
                )
                s.bundle = links.swap(sent, 2)
                slots["p"] = {0: packed, 1: links.swap(packed, 1)}
                return
            (packed,) = call(
                pack_kernel,
                [(pack_shape, BF)],
                proj_weight,
                row(up_bias),
                place,
                base,
                scalars=2,
                name="pack",
            )
            far("p", packed)
            near("p")
            far("d", down_weight)
            near("d")

        def prep():
            s.first, s.first_t = call(
                prep_kernel,
                [((rows, width), BF), ((width, rows), BF)],
                residual_in,
                first_gain,
                first_shift,
                also=[slots["u"][1], slots["d"][1]],
                name="prep",
            )

        def attend_call(which):
            n = len(which)
            for u in which:
                parts = [slots["t"][k] for k in range(u * group, (u + 1) * group)]
                triple_w[u] = parts[0]
                if group > 1:
                    (triple_w[u],) = call(
                        pair_kernel, [((width, 6 * HEAD_DIM), BF)], *parts, name="pair"
                    )
            got = call(
                functools.partial(attend_kernel, n, seqs),
                [((rows, 6 * HEAD_DIM), BF)] * n
                + [((seqs, 2 * SEQ, SEQ), F32)] * n
                + [((rows, 2 * HEAD_DIM), BF)] * n,
                s.first,
                *(triple_w[u] for u in which),
                *scalars,
                scalars=4,
                name="attend",
            )
            for i, u in enumerate(which):
                triples[u], probs[u], mixeds[u] = got[i], got[n + i], got[2 * n + i]

        def project_rows(which):
            for u in which:
                parts = [slots["p"][k] for k in range(u * group, (u + 1) * group)]
                proj_w[u] = parts[0]
                if group > 1:
                    (proj_w[u],) = call(
                        pair_kernel, [((width + 16, 2 * HEAD_DIM), BF)], *parts, name="pair"
                    )

        def cot_low():
            s.out_low, s.out_t = call(
                out_kernel, [((rows, width), BF), ((width, rows), BF)], cotangent, name="out"
            )

        def project():
            project_rows(early)
            (s.acc,) = call(
                functools.partial(project_kernel, len(early)),
                [((rows, width), F32)],
                *(mixeds[u] for u in early),
                *(proj_w[u] for u in early),
                name="project",
            )

        def relay_triple():
            for k in evens:
                relay("t", k)

        def unbundle():
            if shared:
                slots["p"][2], s.half_low = call(
                    unbundle_kernel, [(pack_shape, BF), (half, BF)], s.bundle, name="unbundle"
                )
                slots["p"][3] = links.swap(slots["p"][2], 1)
                s.down_other = links.swap(s.half_low, nslots)
                return
            for k in evens:
                relay("p", k)

        def second():
            project_rows(late)
            s.middle, s.second, s.second_t = call(
                functools.partial(second_kernel, len(late)),
                [((rows, width), F32), ((rows, width), BF), ((width, rows), BF)],
                *(mixeds[u] for u in late),
                *(proj_w[u] for u in late),
                s.acc,
                residual_in,
                proj_bias,
                second_gain,
                second_shift,
                name="second",
            )

        def hidden_call(which):
            n = len(which)
            got = call(
                functools.partial(hidden_kernel, n),
                [((rows, hidden), BF)] * n
                + [((rows, hidden), F32)] * n
                + [((width, hidden), kind(k)) for k in which],
                s.second,
                s.out_t,
                *(slots["u"][k] for k in which),
                *(slots["p"][k] for k in which),
                name="hidden",
            )
            for i, k in enumerate(which):
                acts[k], slopes[k], down_grads[k] = got[i], got[n + i], got[2 * n + i]
                if k != 1:
                    down_sum.give(k, down_grads[k])

        def hidden_back_call(which):
            n, acc = len(which), [s.grad_second] if hasattr(s, "grad_second") else []
            pieces = [thirds if k % 2 and k > 1 else [width] for k in which]
            got = call(
                functools.partial(hidden_back_kernel, [len(p) for p in pieces], not acc),
                [((r, hidden), kind(k)) for k, p in zip(which, pieces) for r in p]
                + [((1, hidden), F32)] * n
                + [((rows, width), F32)],
                s.out_low,
                s.second_t,
                *(slots["u"][k] for k in which),
                *(slots["d"][k] for k in which),
                *(slopes[k] for k in which),
                *acc,
                scratch=[((rows, hidden), BF)] * n,
                name="hidden_back",
            )
            got = list(got)
            for k, p in zip(which, pieces):
                up_grads[k] = [got.pop(0) for _ in p]
                if k != 1:
                    up_sum.give(k, *up_grads[k])
            for k in which:
                biases[k] = got.pop(0)
            s.grad_second = got.pop(0)

        def join_down():
            if shared:
                (slots["d"][2],) = call(
                    functools.partial(join_kernel, 1),
                    [(down_weight.shape, BF)],
                    s.half_low,
                    s.down_other,
                    place,
                    scalars=1,
                    name="join",
                )
                slots["d"][3] = links.swap(slots["d"][2], 1)
                return
            for k in evens:
                relay("d", k)

        def relay_up():
            for k in evens:
                relay("u", k)

        def middle():
            s.grad_middle, s.middle_low, s.middle_t, s.sums_middle = call(
                middle_kernel,
                [((rows, width), F32), ((rows, width), BF), ((width, rows), BF), ((8, width), F32)],
                s.grad_second,
                s.middle,
                second_gain,
                cotangent,
                name="middle",
            )

        def attend_back_call(which):
            n = len(which)
            which_slots = [k for u in which for k in range(group * u, group * (u + 1))]
            pieces = [thirds if k % 2 and k > 1 else [width] for k in which_slots]
            span = 8 * HEAD_DIM // group
            got = call(
                functools.partial(attend_back_kernel, n, group, [len(p) for p in pieces], seqs),
                [((rows, 6 * HEAD_DIM), BF)] * n
                + [((r, span), kind(k)) for k, p in zip(which_slots, pieces) for r in p],
                s.middle_low,
                s.middle_t,
                s.first_t,
                *(proj_w[u] for u in which),
                *(triples[u] for u in which),
                *(probs[u] for u in which),
                *(mixeds[u] for u in which),
                scratch=[((rows, 2 * HEAD_DIM), BF)] * n + [((seqs, 2 * SEQ, SEQ), F32)] * n,
                name="attend_back",
            )
            for i, u in enumerate(which):
                gtls[u] = got[i]
            got = list(got[n:])
            for k, p in zip(which_slots, pieces):
                triple_sum.give(k, *(got.pop(0) for _ in p))

        def heads(chain, spare=False):
            while chain.bit < nslots:
                chain.head(spare=spare)

        def input_grad():
            s.grad_input, s.sums_input = call(
                functools.partial(input_kernel, units),
                [((rows, width), F32, True), ((8, width), F32)],
                *(gtls[u] for u in range(units)),
                *(triple_w[u] for u in range(units)),
                residual_in,
                first_gain,
                s.grad_middle,
                cotangent,
                name="input",
            )

        def vector():
            (s.vector,) = call(
                functools.partial(vector_kernel, [3, 3] + [1] * nslots),
                [((16, width), F32)],
                s.sums_middle,
                s.sums_input,
                *(biases[k] for k in range(nslots)),
                name="vector",
            )
            s.vector_got = links.swap(s.vector, 1)

        def vector_core():
            (triple_sum.rider,) = call(
                functools.partial(vector_core_kernel, nslots, 6),
                [(room, F32)],
                s.vector,
                s.vector_got,
                name="vector_core",
            )

        def halves(chain):
            for bit in middle_bits:
                chain.halve(bit)

        def block():
            (s.block_out,) = call(
                functools.partial(output_kernel, nslots),
                [((rows, width), F32, True)],
                *(acts[k] for k in range(nslots)),
                *(slots["d"][k] for k in range(nslots)),
                s.middle,
                down_bias,
                name="output",
            )

        def settle(chain, order=None):
            chain.settle(order or there[::-1])
            for _ in there[2:]:
                chain.double()

        def settle_triple():
            s.vector = triple_sum.settle(there[::-1])
            for _ in there[2:]:
                triple_sum.double()
            s.vector_bit = 2
            s.vector_got = links.swap(s.vector, 2)

        def finish_triple():
            outs = [(width, 6 * HEAD_DIM // group), (proj_rows, width)], [False, True]
            s.grad_triple, s.grad_proj = triple_sum.finish(*outs)

        def totals():
            while 2 * s.vector_bit < nslots:
                (s.vector,) = call(
                    functools.partial(vector_add_kernel, s.vector_bit // 2, 6),
                    [(room, F32)],
                    s.vector,
                    s.vector_got,
                    name="vector_add",
                )
                s.vector_bit *= 2
                s.vector_got = links.swap(s.vector, s.vector_bit)
            s.totals = call(
                functools.partial(vector_last_kernel, s.vector_bit // 2, 6),
                [((1, width), F32)] * 6 + [((1, hidden), F32)],
                s.vector,
                s.vector_got,
                name="vector_last",
            )

        def finish_down():
            (s.grad_down,) = down_sum.finish([(hidden, width)], [True])

        def finish_up():
            (s.grad_up,) = up_sum.finish([(width, hidden)], [False])

        bundle()
        prep()
        attend_call(early)
        cot_low()
        project()
        relay_triple()
        for u in late:
            attend_call([u])
        unbundle()
        second()
        hidden_call([0, 1])
        hidden_back_call([0, 1])
        join_down()
        relay_up()
        down_sum.give_later(1, down_grads[1])
        up_sum.give_later(1, *up_grads[1])
        for k in evens:
            hidden_call([k])
        for k in odds:
            hidden_call([k])
        down_sum.fold(0)
        up_sum.fold(0)
        for k in evens:
            hidden_back_call([k])
        heads(down_sum, True)
        for k in odds:
            hidden_back_call([k])
        middle()
        for k in evens:
            up_sum.fold(k)
        up_sum.halve(bits[0])
        attend_back_call(late[::-1])
        attend_back_call(early[::-1])
        heads(triple_sum)
        input_grad()
        heads(up_sum)
        down_sum.halve(bits[0])
        vector()
        vector_core()
        halves(down_sum)
        triple_sum.halve(bits[0])
        halves(up_sum)
        down_sum.whole(bits[-1])
        halves(triple_sum)
        triple_sum.whole(bits[-1])
        up_sum.whole(bits[-1])
        block()
        settle(down_sum, there)
        settle_triple()
        settle(up_sum, there)
        down_sum.double()
        triple_sum.double()
        up_sum.double()
        totals()
        finish_down()
        finish_triple()
        finish_up()
        totals = [v.reshape(-1) for v in s.totals]
        return (
            s.block_out,
            s.grad_input,
            s.grad_triple,
            s.grad_proj,
            s.grad_up,
            totals[6],
            s.grad_down,
            totals[0],
            totals[3],
            totals[4],
            totals[5],
            totals[1],
            totals[2],
        )

    return shards


def solution(mesh):
    in_specs = (
        P(("dp", "head"), None),
        P(("dp", "head"), None),
        P(None, "head"),
        P("head", None),
        P(None, "head"),
        P("head"),
        P("head", None),
        P(),
        P(),
        P(),
        P(),
        P(),
        P(),
        P("dp"),
        P("dp"),
        P("dp"),
    )
    out_specs = (
        P(("dp", "head"), None),
        P(("dp", "head"), None),
        P(None, "head"),
        P("head", None),
        P(None, "head"),
        P("head"),
        P("head", None),
        P(),
        P(),
        P(),
        P(),
        P(),
        P(),
    )
    return jax.shard_map(
        make(mesh), mesh=mesh, in_specs=in_specs, out_specs=out_specs, check_vma=False
    )
```

```python
import functools
import types

import jax
import jax.numpy as jnp
from jax import lax
from jax.experimental import pallas as pl
from jax.experimental.pallas import tpu as pltpu
from jax.sharding import PartitionSpec as P

HEAD_DIM = 64
SEQ = 128
EPSILON = 1e-05
NEG_FILL = -1e30
BF = jnp.bfloat16
F32 = jnp.float32
AXES = ("dp", "head")
CHUNK = 128
VMEM_LIMIT = 8 * 2**20


def nn(a, b):
    return lax.dot_general(a, b, (((1,), (0,)), ((), ())), preferred_element_type=F32)


def nt(a, b):
    return lax.dot_general(a, b, (((1,), (1,)), ((), ())), preferred_element_type=F32)


def tn(a, b):
    return lax.dot_general(a, b, (((0,), (0,)), ((), ())), preferred_element_type=F32)


class Kernels:
    def __init__(self):
        self.token = jnp.zeros((8, 128), F32)

    def call(self, body, outs, *args, scalars=0, scratch=(), also=(), name=None):
        vmem = pl.BlockSpec(memory_space=pltpu.VMEM)
        smem = pl.BlockSpec(memory_space=pltpu.SMEM)
        plain, count = len(args) - scalars, len(args)

        mine = count + len(also)
        last = mine + 1 + len(outs)

        def ordered(*refs):
            refs[last][...] = refs[mine][...]
            body(*refs[:count], *refs[mine + 1 : last], *refs[last + 1 :])

        got = pl.pallas_call(
            ordered,
            out_shape=[jax.ShapeDtypeStruct(*out[:2]) for out in outs]
            + [jax.ShapeDtypeStruct((8, 128), F32)],
            in_specs=[vmem] * plain + [smem] * scalars + [vmem] * (len(also) + 1),
            out_specs=[vmem] * (len(outs) + 1),
            compiler_params=pltpu.CompilerParams(vmem_limit_bytes=VMEM_LIMIT),
            scratch_shapes=[pltpu.VMEM(*s) for s in scratch],
            cost_estimate=pl.CostEstimate(flops=0, bytes_accessed=0, transcendentals=0),
            name=name,
        )(*args, *also, self.token)
        self.token = got[-1]
        return got[:-1]


def centred(rows):
    centre = rows - jnp.mean(rows, axis=-1, keepdims=True)
    spread = jnp.mean(centre * centre, axis=-1, keepdims=True)
    rstd = lax.rsqrt(spread + EPSILON)
    return centre * rstd, rstd


def norm_back(grad, rows, gain):
    xhat, rstd = centred(rows)
    q = grad * gain
    inner = jnp.mean(q * xhat, axis=-1, keepdims=True)
    row = rstd * (q - jnp.mean(q, axis=-1, keepdims=True) - xhat * inner)
    return row, jnp.sum(grad * xhat, axis=0, keepdims=True), jnp.sum(grad, axis=0, keepdims=True)


def prep_kernel(res, gain, shift, first, first_t):
    for r in range(0, res.shape[0], CHUNK):
        xhat, _ = centred(res[r : r + CHUNK, :])
        low = (xhat * gain[...] + shift[...]).astype(BF)
        first[r : r + CHUNK, :] = low
        first_t[:, r : r + CHUNK] = low.T


def out_kernel(cot, out_low, out_t):
    for r in range(0, cot.shape[0], CHUNK):
        low = cot[r : r + CHUNK, :].astype(BF)
        out_low[r : r + CHUNK, :] = low
        out_t[:, r : r + CHUNK] = low.T


def lanes_low(shape):
    return lax.broadcasted_iota(jnp.int32, shape, 1) < HEAD_DIM


def half_turn(block):
    return jnp.concatenate([block[:, HEAD_DIM:], block[:, :HEAD_DIM]], 1)


def mask_of(start, count, length):
    m = lax.broadcasted_iota(jnp.int32, (SEQ, SEQ), 0)
    n = lax.broadcasted_iota(jnp.int32, (SEQ, SEQ), 1)
    group_m = jnp.maximum((m * 43) >> 8, start)
    group_n = jnp.maximum((n * 43) >> 8, start)
    seen = (m < length) & ((group_m <= group_n) | (m < count))
    return jnp.where(seen, 0.0, NEG_FILL)


def blocks_of(triple, s):
    at = slice(s * SEQ, (s + 1) * SEQ)
    b0, b1, b2 = (triple[at, c * 128 : (c + 1) * 128] for c in range(3))
    low, zero = lanes_low(b0.shape), jnp.zeros(b0.shape, BF)
    keys = jnp.concatenate([jnp.where(low, zero, b0), jnp.where(low, b2, zero)], 0)
    values = jnp.concatenate([jnp.where(low, b1, zero), jnp.where(low, zero, b2)], 0)
    queries = half_turn(jnp.where(low, b0, b1)) * jnp.asarray(HEAD_DIM**-0.5, BF)
    return keys, values, queries


def attend(first, weight, triple, probs, mixed, scalars, seqs):
    triple[...] = nn(first[...], weight[...]).astype(BF)
    base, starts, counts, lengths = scalars
    parts = [blocks_of(triple, s) for s in range(seqs)]
    for s, (keys, _, queries) in enumerate(parts):
        probs[s] = nt(keys, queries)
    for s in range(seqs):
        bias = mask_of(*(ref[base + s] for ref in (starts, counts, lengths)))
        for h in range(2):
            at = slice(h * SEQ, (h + 1) * SEQ)
            score = probs[s, at, :] + bias
            weights = jnp.exp(score - jnp.max(score, axis=0, keepdims=True))
            probs[s, at, :] = weights * (1.0 / jnp.sum(weights, axis=0, keepdims=True))
    for s, (_, values, _) in enumerate(parts):
        mixed[s * SEQ : (s + 1) * SEQ, :] = tn(probs[s].astype(BF), values).astype(BF)


def attend_back(middle_low, proj, triple, probs, seqs, gtl, grad_mixed, grad_probs):
    grad_mixed[...] = nn(middle_low[...], proj[: middle_low.shape[1], :]).astype(BF)
    parts = [blocks_of(triple, s) for s in range(seqs)]
    spots = [slice(s * SEQ, (s + 1) * SEQ) for s in range(seqs)]
    for s, (_, values, _) in enumerate(parts):
        grad_probs[s] = nt(values, grad_mixed[spots[s], :])
    lows = []
    for s in range(seqs):
        scores = []
        for h in range(2):
            at = slice(h * SEQ, (h + 1) * SEQ)
            prob, grad = probs[s, at, :], grad_probs[s, at, :]
            inner = jnp.sum(grad * prob, axis=0, keepdims=True)
            scores.append((prob * (grad - inner)).astype(BF))
        lows.append(jnp.concatenate(scores, 0))
    low = lanes_low((SEQ, 2 * HEAD_DIM))
    for s, (keys, _, queries) in enumerate(parts):
        grad_queries = half_turn(tn(lows[s], keys) * HEAD_DIM**-0.5)
        grad_keys = nn(lows[s], queries)
        grad_values = nn(probs[s].astype(BF), grad_mixed[spots[s], :])
        gtl[spots[s], 0:128] = jnp.where(low, grad_queries, grad_keys[:SEQ]).astype(BF)
        gtl[spots[s], 128:256] = jnp.where(low, grad_values[:SEQ], grad_queries).astype(BF)
        gtl[spots[s], 256:384] = jnp.where(low, grad_keys[SEQ:], grad_values[SEQ:]).astype(BF)


def gelu_parts(x):
    c0, c1 = 0.7978845608028654, 0.044715
    square = x * x
    t = jnp.tanh(x * (c0 + (c0 * c1) * square))
    h = 0.5 * (1.0 + t)
    slope = h + (0.5 * x) * (1.0 - t * t) * (c0 + (3.0 * c0 * c1) * square)
    return x * h, slope


def pack_kernel(proj, bias, place, base, out, *more):
    deep, span = proj.shape[1], out.shape[1]
    out[:deep, :] = proj[...].T
    rows = bias.shape[1] // span
    out[deep:, :] = jnp.concatenate(
        [bias[:, k * span : (k + 1) * span] for k in range(rows)]
        + [jnp.zeros((16 - rows, span), out.dtype)],
        0,
    )


def bundle_kernel(proj, bias, down, place, base, out, bundle):
    pack_kernel(proj, bias, place, base, out)
    deep, span = out.shape
    bundle[:deep, :] = out[...]
    half, per = down.shape[0] // 2, down.shape[1] // span
    rows = down[pl.ds(pl.multiple_of((place[0] % 2) * half, half), half), :]
    for k in range(per):
        bundle[deep + k * half : deep + (k + 1) * half, :] = rows[:, k * span : (k + 1) * span]


def unbundle_kernel(bundle, out, rows):
    deep, span = out.shape
    out[...] = bundle[:deep, :]
    half = rows.shape[0]
    for k in range(rows.shape[1] // span):
        rows[:, k * span : (k + 1) * span] = bundle[deep + k * half : deep + (k + 1) * half, :]


def pair_kernel(*refs):
    out, col = refs[-1], 0
    for part in refs[:-1]:
        out[:, col : col + part.shape[1]] = part[...]
        col += part.shape[1]


def relay_kernel(value, out):
    out[...] = value[...]


def attend_kernel(units, seqs, *refs):
    refs = list(refs)
    take = lambda n: [refs.pop(0) for _ in range(n)]
    (first,) = take(1)
    weights = take(units)
    scalars = take(4)
    scalars = [scalars[0][0]] + scalars[1:]
    triples, probs, mixeds = take(units), take(units), take(units)
    for u in range(units):
        attend(first, weights[u], triples[u], probs[u], mixeds[u], scalars, seqs)


def project_kernel(units, *refs):
    mixeds, projs, acc = refs[:units], refs[units : 2 * units], refs[2 * units]
    acc[...] = sum(
        nt(mixeds[u][...], projs[u][: acc.shape[1], :]) for u in range(units)
    )


def second_kernel(units, *refs):
    refs = list(refs)
    take = lambda n: [refs.pop(0) for _ in range(n)]
    mixeds, projs = take(units), take(units)
    acc, residual, bias, gain, shift, middle, second, second_t = refs
    for r in range(0, acc.shape[0], CHUNK):
        at = slice(r, r + CHUNK)
        out = acc[at, :] + sum(
            nt(mixeds[u][at, :], projs[u][: acc.shape[1], :]) for u in range(units)
        )
        out = residual[at, :] + out + bias[...]
        middle[at, :] = out
        xhat, _ = centred(out)
        low = (xhat * gain[...] + shift[...]).astype(BF)
        second[at, :] = low
        second_t[:, at] = low.T


def hidden_kernel(slots, *refs):
    refs = list(refs)
    take = lambda n: [refs.pop(0) for _ in range(n)]
    second, out_t = take(2)
    ups, biases = take(slots), take(slots)
    acts, slopes, grads = take(slots), take(slots), take(slots)
    for j in range(slots):
        span, tile = biases[j].shape[1], biases[j][second.shape[1] :, :].astype(F32)
        bias = jnp.concatenate([tile[k : k + 1, :] for k in range(ups[j].shape[1] // span)], 1)
        for r in range(0, second.shape[0], 2 * CHUNK):
            at = slice(r, r + 2 * CHUNK)
            act, slope = gelu_parts(nn(second[at, :], ups[j][...]) + bias)
            acts[j][at, :] = act.astype(BF)
            slopes[j][at, :] = slope
        grads[j][...] = nn(out_t[...], acts[j][...]).astype(grads[j].dtype)


def hidden_back_kernel(pieces, first_call, *refs):
    refs, slots = list(refs), len(pieces)
    take = lambda n: [refs.pop(0) for _ in range(n)]
    out_low, second_t = take(2)
    ups, downs, slopes = take(slots), take(slots), take(slots)
    acc_in = None if first_call else take(1)[0]
    grads, biases = [take(n) for n in pieces], take(slots)
    (acc,) = take(1)
    pre = take(slots)
    for j in range(slots):
        total = 0.0
        for r in range(0, out_low.shape[0], 2 * CHUNK):
            at = slice(r, r + 2 * CHUNK)
            low = (nt(out_low[at, :], downs[j][...]) * slopes[j][at, :]).astype(BF)
            pre[j][at, :] = low
            total = total + jnp.sum(low.astype(F32), axis=0, keepdims=True)
        biases[j][...] = total
        grad, first = nn(second_t[...], pre[j][...]), 0
        for out in grads[j]:
            out[...] = grad[first : first + out.shape[0], :].astype(out.dtype)
            first += out.shape[0]
    for r in range(0, out_low.shape[0], 2 * CHUNK):
        at = slice(r, r + 2 * CHUNK)
        out = sum(nt(pre[j][at, :], ups[j][...]) for j in range(slots))
        acc[at, :] = out if first_call else acc_in[at, :] + out


def middle_kernel(grad_second, middle, gain, cot, grad_middle, middle_low, middle_t, sums):
    totals = [0.0, 0.0, 0.0]
    for r in range(0, cot.shape[0], CHUNK):
        at = slice(r, r + CHUNK)
        row, dgain, dshift = norm_back(grad_second[at, :], middle[at, :], gain[...])
        grad = cot[at, :] + row
        grad_middle[at, :] = grad
        low = grad.astype(BF)
        middle_low[at, :] = low
        middle_t[:, at] = low.T
        parts = (jnp.sum(grad, axis=0, keepdims=True), dgain, dshift)
        totals = [t + p for t, p in zip(totals, parts)]
    for i, t in enumerate(totals):
        sums[i : i + 1, :] = t


def attend_back_kernel(units, group, pieces, seqs, *refs):
    refs = list(refs)
    take = lambda n: [refs.pop(0) for _ in range(n)]
    middle_low, middle_t, first_t = take(3)
    projs, triples, probs, mixeds = take(units), take(units), take(units), take(units)
    gtls, grads = take(units), [take(n) for n in pieces]
    grad_mixed, grad_probs = take(units), take(units)
    span, small = 6 * HEAD_DIM // group, 2 * HEAD_DIM // group
    for u in range(units):
        attend_back(
            middle_low,
            projs[u],
            triples[u],
            probs[u],
            seqs,
            gtls[u],
            grad_mixed[u],
            grad_probs[u],
        )
        grad = nn(first_t[...], gtls[u][...])
        proj_grad = nn(middle_t[...], mixeds[u][...])
        for k in range(group):
            first = 0
            for out in grads[u * group + k]:
                at = slice(first, first + out.shape[0])
                first += out.shape[0]
                out[:, :span] = grad[at, k * span : (k + 1) * span].astype(out.dtype)
                out[:, span:] = proj_grad[at, k * small : (k + 1) * small].astype(out.dtype)


def input_kernel(units, *refs):
    refs = list(refs)
    take = lambda n: [refs.pop(0) for _ in range(n)]
    gtls, weights = take(units), take(units)
    residual, gain, grad_middle, cot = take(4)
    grad_input, sums = take(2)
    totals = [0.0, 0.0, 0.0]
    for r in range(0, cot.shape[0], CHUNK):
        at = slice(r, r + CHUNK)
        grad = sum(nt(gtls[u][at, :], weights[u][...]) for u in range(units))
        row, dgain, dshift = norm_back(grad, residual[at, :], gain[...])
        grad_input[at, :] = grad_middle[at, :] + row
        parts = (jnp.sum(cot[at, :], axis=0, keepdims=True), dgain, dshift)
        totals = [t + p for t, p in zip(totals, parts)]
    for i, t in enumerate(totals):
        sums[i : i + 1, :] = t


def output_kernel(slots, *refs):
    acts, downs = refs[:slots], refs[slots : 2 * slots]
    middle, bias, out = refs[2 * slots :]
    for r in range(0, middle.shape[0], 2 * CHUNK):
        at = slice(r, r + 2 * CHUNK)
        total = sum(nn(acts[j][at, :], downs[j][...]) for j in range(slots))
        out[at, :] = middle[at, :] + total + bias[...]


def total(terms):
    out = terms[0]
    for term in terms[1:]:
        out = out + term
    return out


def read(refs, spots, at):
    terms = []
    for where, first in spots:
        if len(where) > 1:
            terms.append(jnp.concatenate([refs[i][...] for i in where], 0).astype(F32))
        else:
            terms.append(refs[where[0]][pl.ds(first + at[0], at[1]), :].astype(F32))
    return total(terms)


def rider_rows(rider, cols):
    return 2 * rider[0] * -(-(rider[1] // 128) // max(1, cols // 128))


def pack_rider(rider, out, first):
    per, deep = max(1, out.shape[1] // 128), 2 * rider.shape[0]
    high = rider.astype(BF)
    rest = (rider - high.astype(F32)).astype(BF)
    for j in range(rider.shape[1] // 128):
        at, row, col = slice(j * 128, (j + 1) * 128), first + deep * (j // per), 128 * (j % per)
        block = jnp.concatenate([high[:, at], rest[:, at]], 0)
        out[row : row + deep, col : col + 128] = block


def unpack_rider(value, first, shape):
    rows, per, parts = shape[0], max(1, value.shape[1] // 128), []
    for j in range(shape[1] // 128):
        row, col = first + 2 * rows * (j // per), 128 * (j % per)
        block = value[row : row + 2 * rows, col : col + 128].astype(F32)
        parts.append(block[:rows, :] + block[rows:, :])
    return jnp.concatenate(parts, 1)


def rider_total(refs, ride):
    kept, came, first = ride
    rider = refs[kept][...]
    for i in came:
        rider = rider + unpack_rider(refs[i], first, rider.shape)
    return rider


def send_kernel(spots, rows, *refs):
    count = 1 + max(i for spot in spots for where, _ in spot for i in where)
    outs = refs[count:]
    if len(outs) > 1:
        value = read(refs, spots[0], (0, rows)).astype(BF)
        for k, out in enumerate(outs):
            out[...] = value[k * out.shape[0] : (k + 1) * out.shape[0], :]
        return
    (out,) = outs
    used = len(spots) * rows
    for k, spot in enumerate(spots):
        out[k * rows : (k + 1) * rows, :] = read(refs, spot, (0, rows)).astype(out.dtype)
    if used < out.shape[0]:
        out[used:, :] = jnp.zeros((out.shape[0] - used, out.shape[1]), out.dtype)


def halve_kernel(spots, rows, bit, ride, *refs):
    refs = list(refs)
    if ride:
        rider_keep = refs.pop()
    send = refs.pop()
    stays = [refs.pop() for _ in spots][::-1]
    place = refs.pop()
    half = rows // 2
    mine = (place[0] // bit) % 2
    for k, spot in enumerate(spots):
        stays[k][...] = read(refs, spot, (pl.multiple_of(mine * half, half), half))
        leave = read(refs, spot, (pl.multiple_of((1 - mine) * half, half), half))
        send[k * half : (k + 1) * half, :] = leave.astype(BF)
    room = len(spots) * half
    if room < send.shape[0]:
        send[room:, :] = jnp.zeros((send.shape[0] - room, send.shape[1]), BF)
    if ride:
        rider = rider_total(refs, ride)
        rider_keep[...] = rider
        pack_rider(rider, send, len(spots) * half)


def whole_kernel(spots, rows, ride, *refs):
    refs = list(refs)
    if ride:
        rider_keep = refs.pop()
    send, keep = refs.pop(), refs.pop()
    value = read(refs, spots[0], (0, rows))
    keep[...] = value
    send[:rows, :] = value.astype(BF)
    send[rows:, :] = jnp.zeros((send.shape[0] - rows, send.shape[1]), BF)
    if ride:
        rider = rider_total(refs, ride)
        rider_keep[...] = rider
        pack_rider(rider, send, rows)


def settle_kernel(spots, rows, ride, *refs):
    refs = list(refs)
    if ride:
        rider_out = refs.pop()
    out = refs.pop()
    out[...] = read(refs, spots[0], (0, rows)).astype(out.dtype)
    if ride:
        rider_out[...] = rider_total(refs, ride)


def join_kernel(bit, own, other, place, out):
    half = own.shape[0]
    mine = (place[0] // bit) % 2
    out[pl.ds(pl.multiple_of(mine * half, half), half), :] = own[...].astype(out.dtype)
    out[pl.ds(pl.multiple_of((1 - mine) * half, half), half), :] = other[...].astype(out.dtype)


def finish_kernel(bit, blocks, turned, own, other, place, *refs):
    outs, low = refs[:-1], refs[-1]
    join_kernel(bit, own, other, place, low)
    rows, col = low.shape[0] // len(blocks), 0
    for out, turn in zip(outs, turned):
        span = out.shape[0] if turn else out.shape[1]
        for to, at in enumerate(blocks):
            part = low[at * rows : (at + 1) * rows, col : col + span]
            if turn:
                out[:, to * rows : (to + 1) * rows] = part.T
            else:
                out[to * rows : (to + 1) * rows, :] = part
        col += span


def vector_kernel(parts, *refs):
    out = refs[-1]
    out[...] = jnp.zeros_like(out)
    row = 0
    for ref, n in zip(refs, parts):
        out[row : row + n, : ref.shape[1]] = ref[:n, :]
        row += n


def vector_core_kernel(heads, fixed, mine, got, out):
    out[...] = jnp.zeros_like(out)
    out[:fixed, :] = mine[:fixed, :] + got[:fixed, :]
    for k in range(0, heads, 2):
        at, other, to = fixed + k, fixed + k + 1, fixed + k // 2
        out[to : to + 1, :] = mine[at : at + 1, :] + got[other : other + 1, :]


def vector_add_kernel(bit, fixed, mine, got, out):
    out[...] = mine[...] + got[...]
    for k in range(out.shape[0] - fixed):
        if k ^ bit < out.shape[0] - fixed:
            at, other = fixed + k, fixed + (k ^ bit)
            out[at : at + 1, :] = mine[at : at + 1, :] + got[other : other + 1, :]


def vector_last_kernel(bit, fixed, mine, got, *outs):
    for k in range(fixed + 1):
        other, span = (k if k < fixed else fixed + bit), outs[k].shape[1]
        outs[k][...] = mine[k : k + 1, :span] + got[other : other + 1, :span]


class Links:
    def __init__(self, mesh):
        self.dp, self.head = mesh.shape["dp"], mesh.shape["head"]

    def swap(self, value, bit):
        total = self.dp * self.head
        return lax.ppermute(value, AXES, [(i, i ^ bit) for i in range(total)])


class Chain:
    def __init__(self, links, kernels, place, room, tag):
        self.tag = tag
        self.room = room
        self.links, self.kernels, self.place = links, kernels, place
        self.slots, self.bit, self.halved = {}, 2, []
        self.rider, self.rider_came = None, []
        self.rider_first = 0

    def give(self, slot, *values):
        self.rows, self.cols = sum(v.shape[0] for v in values), values[0].shape[1]
        if slot % 2:
            got = [self.links.swap(v, 1) for v in values]
            self.slots.setdefault(slot - 1, []).insert(0, (got, 0))
        else:
            self.slots.setdefault(slot, []).insert(0, (list(values), 0))

    def give_later(self, slot, value):
        (value,) = self.kernels.call(relay_kernel, [(value.shape, BF)], value, name="relay")
        self.give(slot, value)

    def spots(self, sums):
        arrays, spots = [], []
        for terms in sums:
            spots.append([])
            for values, first in terms:
                where = []
                for value in values:
                    known = [i for i, a in enumerate(arrays) if a is value]
                    if not known:
                        arrays.append(value)
                        known = [len(arrays) - 1]
                    where.append(known[0])
                spots[-1].append((where, first))
        return arrays, spots

    def head(self, pieces=1, spare=False):
        leave = [k for k in self.slots if k & self.bit]
        arrays, spots = self.spots([self.slots[k] for k in leave])
        room = rider_rows(self.room, self.cols) if self.halved or spare else 0
        deep = len(leave) * self.rows + room
        sends = self.kernels.call(
            functools.partial(send_kernel, spots, self.rows),
            [((deep // pieces, self.cols), BF)] * pieces,
            *arrays,
            name="send_" + self.tag,
        )
        got = [self.links.swap(send, self.bit) for send in sends]
        for i, k in enumerate(leave):
            del self.slots[k]
            self.slots.setdefault(k ^ self.bit, []).append((got, i * self.rows))
        self.bit *= 2

    def fold(self, slot, count=2):
        arrays, spots = self.spots([self.slots[slot][:count]])
        (value,) = self.kernels.call(
            functools.partial(send_kernel, spots, self.rows),
            [((self.rows, self.cols), F32)],
            *arrays,
            name="fold_" + self.tag,
        )
        self.slots[slot][:count] = [([value], 0)]

    def ride(self, arrays):
        if self.rider is None:
            return None
        arrays.append(self.rider)
        came = [i for i, a in enumerate(arrays) if any(a is b for b in self.rider_came)]
        return len(arrays) - 1, came, self.rider_first

    def rode(self, kept, came, first):
        if self.rider is not None:
            self.rider, self.rider_came, self.rider_first = kept, came, first

    def halve(self, bit):
        keys = list(self.slots)
        arrays, spots = self.spots([self.slots[k] for k in keys])
        half = self.rows // 2
        ride = self.ride(arrays)
        rider = [(self.rider.shape, F32)] if ride else []
        more = rider_rows(self.room, self.cols) if self.halved or len(keys) == 1 else 0
        got = self.kernels.call(
            functools.partial(halve_kernel, spots, self.rows, bit, ride),
            [((half, self.cols), F32)] * len(keys)
            + [((len(keys) * half + more, self.cols), BF)]
            + rider,
            *arrays,
            self.place,
            scalars=1,
            name="halve_" + self.tag,
        )
        came = self.links.swap(got[len(keys)], bit * self.links.head)
        self.slots = {k: [([got[i]], 0), ([came], i * half)] for i, k in enumerate(keys)}
        self.rode(got[-1], [came], len(keys) * half)
        self.rows = half
        self.halved.append(bit)

    def whole(self, bit):
        arrays, spots = self.spots([self.slots[0]])
        ride = self.ride(arrays)
        rider = [(self.rider.shape, F32)] if ride else []
        more = rider_rows(self.room, self.cols)
        got = self.kernels.call(
            functools.partial(whole_kernel, spots, self.rows, ride),
            [((self.rows, self.cols), F32), ((self.rows + more, self.cols), BF)] + rider,
            *arrays,
            name="whole_" + self.tag,
        )
        came = self.links.swap(got[1], bit * self.links.head)
        self.slots = {0: [([got[0]], 0), ([came], 0)]}
        self.rode(got[-1], [came], self.rows)

    def settle(self, order):
        arrays, spots = self.spots([self.slots[0]])
        ride = self.ride(arrays)
        got = self.kernels.call(
            functools.partial(settle_kernel, spots, self.rows, ride),
            [((self.rows, self.cols), BF)] + ([(self.rider.shape, F32)] if ride else []),
            *arrays,
            name="settle_" + self.tag,
        )
        self.own, self.order, self.left = got[0], list(order), list(order)
        self.back()
        return got[-1]

    def back(self):
        self.last = self.left.pop(0)
        self.got = self.links.swap(self.own, self.last * self.links.head)

    def double(self):
        if not self.left:
            return
        self.rows *= 2
        (self.own,) = self.kernels.call(
            functools.partial(join_kernel, self.last),
            [((self.rows, self.cols), BF)],
            self.own,
            self.got,
            self.place,
            scalars=1,
            name="join_" + self.tag,
        )
        self.back()

    def finish(self, outs, turned):
        blocks = []
        for to in range(2 ** len(self.order)):
            digits = {b: to >> (len(self.halved) - 1 - i) & 1 for i, b in enumerate(self.halved)}
            blocks.append(sum(digits[b] << i for i, b in enumerate(self.order)))
        if blocks == sorted(blocks):
            blocks = [0]
        return self.kernels.call(
            functools.partial(finish_kernel, self.last, blocks, turned),
            [(o, F32, True) for o in outs],
            self.own,
            self.got,
            self.place,
            scalars=1,
            scratch=[((2 * self.rows, self.cols), F32)],
            name="finish_" + self.tag,
        )


def make(mesh):
    links = Links(mesh)
    nslots = links.head
    bits = [2**k for k in range(links.dp.bit_length() - 1)]

    def shards(
        residual_in,
        cotangent,
        triple_weight,
        proj_weight,
        up_weight,
        up_bias,
        down_weight,
        proj_bias,
        down_bias,
        first_gain,
        first_shift,
        second_gain,
        second_shift,
        start_steps,
        cond_counts,
        valid_lengths,
    ):
        kernels = Kernels()
        call = kernels.call
        rows, width = residual_in.shape
        seqs = rows // SEQ
        hidden, proj_rows = up_weight.shape[1], proj_weight.shape[0]
        row = lambda v: v.reshape(1, -1)
        proj_bias, down_bias, first_gain, first_shift, second_gain, second_shift = map(
            row, (proj_bias, down_bias, first_gain, first_shift, second_gain, second_shift)
        )
        place = lax.axis_index("dp").astype(jnp.int32).reshape(1)
        base = (lax.axis_index("head") * seqs).astype(jnp.int32).reshape(1)
        scalars = (base, start_steps, cond_counts, valid_lengths)
        group = 2 * HEAD_DIM // proj_rows
        units = nslots // group

        slots = {}

        def far(key, value):
            known = {0: value}
            bit = nslots // 2
            while bit > 1:
                known.update({k | bit: links.swap(v, bit) for k, v in list(known.items())})
                bit //= 2
            slots[key] = known

        def near(key):
            slots[key][1] = links.swap(slots[key][0], 1)

        def relay(key, k):
            value = slots[key][k]
            (value,) = call(relay_kernel, [(value.shape, BF)], value, name="relay")
            slots[key][k + 1] = links.swap(value, 1)

        far("t", triple_weight)
        near("t")
        far("u", up_weight)
        near("u")
        slots["d"] = {0: down_weight, 1: links.swap(down_weight, 1)}
        shared = nslots == 4 and len(bits) > 1
        pack_shape = (width + 16, proj_rows)
        half = (down_weight.shape[0] // 2, width)
        evens, odds = range(2, nslots, 2), range(3, nslots, 2)
        early = list(range(max(1, 2 // group)))
        late = [u for u in range(units) if u not in early]
        triple_w, proj_w, triples, probs, mixeds = {}, {}, {}, {}, {}
        acts, slopes, biases, down_grads, up_grads = {}, {}, {}, {}, {}
        gtls, triple_grads = {}, {}
        room = (8 * -(-(6 + nslots // 2) // 8), width)
        down_sum, up_sum, triple_sum = (Chain(links, kernels, place, room, t) for t in "dut")
        middle_bits, there = bits[1:-1], bits[:-1]
        s = types.SimpleNamespace()
        thirds = [width // 48 * 16 + 16] * 2
        thirds = thirds + [width - sum(thirds)]

        def kind(k):
            return BF if k % 2 else F32

        def bundle():
            if shared:
                deep = pack_shape[0] + half[0] * width // proj_rows
                packed, sent = call(
                    bundle_kernel,
                    [(pack_shape, BF), ((deep, proj_rows), BF)],
                    proj_weight,
                    row(up_bias),
                    down_weight,
                    place,
                    base,
                    scalars=2,
                    name="bundle",
                )
                s.bundle = links.swap(sent, 2)
                slots["p"] = {0: packed, 1: links.swap(packed, 1)}
                return
            (packed,) = call(
                pack_kernel,
                [(pack_shape, BF)],
                proj_weight,
                row(up_bias),
                place,
                base,
                scalars=2,
                name="pack",
            )
            far("p", packed)
            near("p")
            far("d", down_weight)
            near("d")

        def prep():
            s.first, s.first_t = call(
                prep_kernel,
                [((rows, width), BF), ((width, rows), BF)],
                residual_in,
                first_gain,
                first_shift,
                also=[slots["u"][1], slots["d"][1]],
                name="prep",
            )

        def attend_call(which):
            n = len(which)
            for u in which:
                parts = [slots["t"][k] for k in range(u * group, (u + 1) * group)]
                triple_w[u] = parts[0]
                if group > 1:
                    (triple_w[u],) = call(
                        pair_kernel, [((width, 6 * HEAD_DIM), BF)], *parts, name="pair"
                    )
            got = call(
                functools.partial(attend_kernel, n, seqs),
                [((rows, 6 * HEAD_DIM), BF)] * n
                + [((seqs, 2 * SEQ, SEQ), F32)] * n
                + [((rows, 2 * HEAD_DIM), BF)] * n,
                s.first,
                *(triple_w[u] for u in which),
                *scalars,
                scalars=4,
                name="attend",
            )
            for i, u in enumerate(which):
                triples[u], probs[u], mixeds[u] = got[i], got[n + i], got[2 * n + i]

        def project_rows(which):
            for u in which:
                parts = [slots["p"][k] for k in range(u * group, (u + 1) * group)]
                proj_w[u] = parts[0]
                if group > 1:
                    (proj_w[u],) = call(
                        pair_kernel, [((width + 16, 2 * HEAD_DIM), BF)], *parts, name="pair"
                    )

        def cot_low():
            s.out_low, s.out_t = call(
                out_kernel, [((rows, width), BF), ((width, rows), BF)], cotangent, name="out"
            )

        def project():
            project_rows(early)
            (s.acc,) = call(
                functools.partial(project_kernel, len(early)),
                [((rows, width), F32)],
                *(mixeds[u] for u in early),
                *(proj_w[u] for u in early),
                name="project",
            )

        def relay_triple():
            for k in evens:
                relay("t", k)

        def unbundle():
            if shared:
                slots["p"][2], s.half_low = call(
                    unbundle_kernel, [(pack_shape, BF), (half, BF)], s.bundle, name="unbundle"
                )
                slots["p"][3] = links.swap(slots["p"][2], 1)
                s.down_other = links.swap(s.half_low, nslots)
                return
            for k in evens:
                relay("p", k)

        def second():
            project_rows(late)
            s.middle, s.second, s.second_t = call(
                functools.partial(second_kernel, len(late)),
                [((rows, width), F32), ((rows, width), BF), ((width, rows), BF)],
                *(mixeds[u] for u in late),
                *(proj_w[u] for u in late),
                s.acc,
                residual_in,
                proj_bias,
                second_gain,
                second_shift,
                name="second",
            )

        def hidden_call(which):
            n = len(which)
            got = call(
                functools.partial(hidden_kernel, n),
                [((rows, hidden), BF)] * n
                + [((rows, hidden), F32)] * n
                + [((width, hidden), kind(k)) for k in which],
                s.second,
                s.out_t,
                *(slots["u"][k] for k in which),
                *(slots["p"][k] for k in which),
                name="hidden",
            )
            for i, k in enumerate(which):
                acts[k], slopes[k], down_grads[k] = got[i], got[n + i], got[2 * n + i]
                if k != 1:
                    down_sum.give(k, down_grads[k])

        def hidden_back_call(which):
            n, acc = len(which), [s.grad_second] if hasattr(s, "grad_second") else []
            pieces = [thirds if k % 2 and k > 1 else [width] for k in which]
            got = call(
                functools.partial(hidden_back_kernel, [len(p) for p in pieces], not acc),
                [((r, hidden), kind(k)) for k, p in zip(which, pieces) for r in p]
                + [((1, hidden), F32)] * n
                + [((rows, width), F32)],
                s.out_low,
                s.second_t,
                *(slots["u"][k] for k in which),
                *(slots["d"][k] for k in which),
                *(slopes[k] for k in which),
                *acc,
                scratch=[((rows, hidden), BF)] * n,
                name="hidden_back",
            )
            got = list(got)
            for k, p in zip(which, pieces):
                up_grads[k] = [got.pop(0) for _ in p]
                if k != 1:
                    up_sum.give(k, *up_grads[k])
            for k in which:
                biases[k] = got.pop(0)
            s.grad_second = got.pop(0)

        def join_down():
            if shared:
                (slots["d"][2],) = call(
                    functools.partial(join_kernel, 1),
                    [(down_weight.shape, BF)],
                    s.half_low,
                    s.down_other,
                    place,
                    scalars=1,
                    name="join",
                )
                slots["d"][3] = links.swap(slots["d"][2], 1)
                return
            for k in evens:
                relay("d", k)

        def relay_up():
            for k in evens:
                relay("u", k)

        def middle():
            s.grad_middle, s.middle_low, s.middle_t, s.sums_middle = call(
                middle_kernel,
                [((rows, width), F32), ((rows, width), BF), ((width, rows), BF), ((8, width), F32)],
                s.grad_second,
                s.middle,
                second_gain,
                cotangent,
                name="middle",
            )

        def attend_back_call(which):
            n = len(which)
            which_slots = [k for u in which for k in range(group * u, group * (u + 1))]
            pieces = [thirds if k % 2 and k > 1 else [width] for k in which_slots]
            span = 8 * HEAD_DIM // group
            got = call(
                functools.partial(attend_back_kernel, n, group, [len(p) for p in pieces], seqs),
                [((rows, 6 * HEAD_DIM), BF)] * n
                + [((r, span), kind(k)) for k, p in zip(which_slots, pieces) for r in p],
                s.middle_low,
                s.middle_t,
                s.first_t,
                *(proj_w[u] for u in which),
                *(triples[u] for u in which),
                *(probs[u] for u in which),
                *(mixeds[u] for u in which),
                scratch=[((rows, 2 * HEAD_DIM), BF)] * n + [((seqs, 2 * SEQ, SEQ), F32)] * n,
                name="attend_back",
            )
            for i, u in enumerate(which):
                gtls[u] = got[i]
            got = list(got[n:])
            for k, p in zip(which_slots, pieces):
                triple_sum.give(k, *(got.pop(0) for _ in p))

        def heads(chain, spare=False):
            while chain.bit < nslots:
                chain.head(spare=spare)

        def input_grad():
            s.grad_input, s.sums_input = call(
                functools.partial(input_kernel, units),
                [((rows, width), F32, True), ((8, width), F32)],
                *(gtls[u] for u in range(units)),
                *(triple_w[u] for u in range(units)),
                residual_in,
                first_gain,
                s.grad_middle,
                cotangent,
                name="input",
            )

        def vector():
            (s.vector,) = call(
                functools.partial(vector_kernel, [3, 3] + [1] * nslots),
                [((16, width), F32)],
                s.sums_middle,
                s.sums_input,
                *(biases[k] for k in range(nslots)),
                name="vector",
            )
            s.vector_got = links.swap(s.vector, 1)

        def vector_core():
            (triple_sum.rider,) = call(
                functools.partial(vector_core_kernel, nslots, 6),
                [(room, F32)],
                s.vector,
                s.vector_got,
                name="vector_core",
            )

        def halves(chain):
            for bit in middle_bits:
                chain.halve(bit)

        def block():
            (s.block_out,) = call(
                functools.partial(output_kernel, nslots),
                [((rows, width), F32, True)],
                *(acts[k] for k in range(nslots)),
                *(slots["d"][k] for k in range(nslots)),
                s.middle,
                down_bias,
                name="output",
            )

        def settle(chain, order=None):
            chain.settle(order or there[::-1])
            for _ in there[2:]:
                chain.double()

        def settle_triple():
            s.vector = triple_sum.settle(there[::-1])
            for _ in there[2:]:
                triple_sum.double()
            s.vector_bit = 2
            s.vector_got = links.swap(s.vector, 2)

        def finish_triple():
            outs = [(width, 6 * HEAD_DIM // group), (proj_rows, width)], [False, True]
            s.grad_triple, s.grad_proj = triple_sum.finish(*outs)

        def totals():
            while 2 * s.vector_bit < nslots:
                (s.vector,) = call(
                    functools.partial(vector_add_kernel, s.vector_bit // 2, 6),
                    [(room, F32)],
                    s.vector,
                    s.vector_got,
                    name="vector_add",
                )
                s.vector_bit *= 2
                s.vector_got = links.swap(s.vector, s.vector_bit)
            s.totals = call(
                functools.partial(vector_last_kernel, s.vector_bit // 2, 6),
                [((1, width), F32)] * 6 + [((1, hidden), F32)],
                s.vector,
                s.vector_got,
                name="vector_last",
            )

        def finish_down():
            (s.grad_down,) = down_sum.finish([(hidden, width)], [True])

        def finish_up():
            (s.grad_up,) = up_sum.finish([(width, hidden)], [False])

        bundle()
        prep()
        attend_call(early)
        cot_low()
        project()
        relay_triple()
        for u in late:
            attend_call([u])
        unbundle()
        second()
        hidden_call([0, 1])
        join_down()
        hidden_back_call([0, 1])
        down_sum.give_later(1, down_grads[1])
        relay_up()
        up_sum.give_later(1, *up_grads[1])
        down_sum.fold(0)
        for k in odds:
            hidden_call([k])
        for k in odds:
            hidden_back_call([k])
        for k in evens:
            hidden_call([k])
        up_sum.fold(0)
        heads(down_sum, True)
        for k in evens:
            hidden_back_call([k])
        middle()
        for k in evens:
            up_sum.fold(k)
        up_sum.halve(bits[0])
        attend_back_call(late[::-1])
        attend_back_call(early[::-1])
        heads(triple_sum)
        input_grad()
        heads(up_sum)
        down_sum.halve(bits[0])
        vector()
        halves(down_sum)
        vector_core()
        triple_sum.halve(bits[0])
        halves(up_sum)
        halves(triple_sum)
        down_sum.whole(bits[-1])
        triple_sum.whole(bits[-1])
        block()
        settle(down_sum, there)
        up_sum.whole(bits[-1])
        settle_triple()
        settle(up_sum, there)
        down_sum.double()
        triple_sum.double()
        up_sum.double()
        totals()
        finish_down()
        finish_triple()
        finish_up()
        totals = [v.reshape(-1) for v in s.totals]
        return (
            s.block_out,
            s.grad_input,
            s.grad_triple,
            s.grad_proj,
            s.grad_up,
            totals[6],
            s.grad_down,
            totals[0],
            totals[3],
            totals[4],
            totals[5],
            totals[1],
            totals[2],
        )

    return shards


def solution(mesh):
    in_specs = (
        P(("dp", "head"), None),
        P(("dp", "head"), None),
        P(None, "head"),
        P("head", None),
        P(None, "head"),
        P("head"),
        P("head", None),
        P(),
        P(),
        P(),
        P(),
        P(),
        P(),
        P("dp"),
        P("dp"),
        P("dp"),
    )
    out_specs = (
        P(("dp", "head"), None),
        P(("dp", "head"), None),
        P(None, "head"),
        P("head", None),
        P(None, "head"),
        P("head"),
        P("head", None),
        P(),
        P(),
        P(),
        P(),
        P(),
        P(),
    )
    return jax.shard_map(
        make(mesh), mesh=mesh, in_specs=in_specs, out_specs=out_specs, check_vma=False
    )
```

```python
import functools
import types

import jax
import jax.numpy as jnp
from jax import lax
from jax.experimental import pallas as pl
from jax.experimental.pallas import tpu as pltpu
from jax.sharding import PartitionSpec as P

HEAD_DIM = 64
SEQ = 128
EPSILON = 1e-05
NEG_FILL = -1e30
BF = jnp.bfloat16
F32 = jnp.float32
AXES = ("dp", "head")
CHUNK = 128
VMEM_LIMIT = 8 * 2**20


def nn(a, b):
    return lax.dot_general(a, b, (((1,), (0,)), ((), ())), preferred_element_type=F32)


def nt(a, b):
    return lax.dot_general(a, b, (((1,), (1,)), ((), ())), preferred_element_type=F32)


def tn(a, b):
    return lax.dot_general(a, b, (((0,), (0,)), ((), ())), preferred_element_type=F32)


class Kernels:
    def __init__(self):
        self.token = jnp.zeros((8, 128), F32)

    def call(self, body, outs, *args, scalars=0, scratch=(), also=(), name=None):
        vmem = pl.BlockSpec(memory_space=pltpu.VMEM)
        smem = pl.BlockSpec(memory_space=pltpu.SMEM)
        plain, count = len(args) - scalars, len(args)

        mine = count + len(also)
        last = mine + 1 + len(outs)

        def ordered(*refs):
            refs[last][...] = refs[mine][...]
            body(*refs[:count], *refs[mine + 1 : last], *refs[last + 1 :])

        got = pl.pallas_call(
            ordered,
            out_shape=[jax.ShapeDtypeStruct(*out[:2]) for out in outs]
            + [jax.ShapeDtypeStruct((8, 128), F32)],
            in_specs=[vmem] * plain + [smem] * scalars + [vmem] * (len(also) + 1),
            out_specs=[vmem] * (len(outs) + 1),
            compiler_params=pltpu.CompilerParams(vmem_limit_bytes=VMEM_LIMIT),
            scratch_shapes=[pltpu.VMEM(*s) for s in scratch],
            cost_estimate=pl.CostEstimate(flops=0, bytes_accessed=0, transcendentals=0),
            name=name,
        )(*args, *also, self.token)
        self.token = got[-1]
        return got[:-1]


def centred(rows):
    centre = rows - jnp.mean(rows, axis=-1, keepdims=True)
    spread = jnp.mean(centre * centre, axis=-1, keepdims=True)
    rstd = lax.rsqrt(spread + EPSILON)
    return centre * rstd, rstd


def norm_back(grad, rows, gain):
    xhat, rstd = centred(rows)
    q = grad * gain
    inner = jnp.mean(q * xhat, axis=-1, keepdims=True)
    row = rstd * (q - jnp.mean(q, axis=-1, keepdims=True) - xhat * inner)
    return row, jnp.sum(grad * xhat, axis=0, keepdims=True), jnp.sum(grad, axis=0, keepdims=True)


def prep_kernel(res, gain, shift, first, first_t):
    for r in range(0, res.shape[0], CHUNK):
        xhat, _ = centred(res[r : r + CHUNK, :])
        low = (xhat * gain[...] + shift[...]).astype(BF)
        first[r : r + CHUNK, :] = low
        first_t[:, r : r + CHUNK] = low.T


def out_kernel(cot, out_low, out_t):
    for r in range(0, cot.shape[0], CHUNK):
        low = cot[r : r + CHUNK, :].astype(BF)
        out_low[r : r + CHUNK, :] = low
        out_t[:, r : r + CHUNK] = low.T


def lanes_low(shape):
    return lax.broadcasted_iota(jnp.int32, shape, 1) < HEAD_DIM


def half_turn(block):
    return jnp.concatenate([block[:, HEAD_DIM:], block[:, :HEAD_DIM]], 1)


def mask_of(start, count, length):
    m = lax.broadcasted_iota(jnp.int32, (SEQ, SEQ), 0)
    n = lax.broadcasted_iota(jnp.int32, (SEQ, SEQ), 1)
    group_m = jnp.maximum((m * 43) >> 8, start)
    group_n = jnp.maximum((n * 43) >> 8, start)
    seen = (m < length) & ((group_m <= group_n) | (m < count))
    return jnp.where(seen, 0.0, NEG_FILL)


def blocks_of(triple, s):
    at = slice(s * SEQ, (s + 1) * SEQ)
    b0, b1, b2 = (triple[at, c * 128 : (c + 1) * 128] for c in range(3))
    low, zero = lanes_low(b0.shape), jnp.zeros(b0.shape, BF)
    keys = jnp.concatenate([jnp.where(low, zero, b0), jnp.where(low, b2, zero)], 0)
    values = jnp.concatenate([jnp.where(low, b1, zero), jnp.where(low, zero, b2)], 0)
    queries = half_turn(jnp.where(low, b0, b1)) * jnp.asarray(HEAD_DIM**-0.5, BF)
    return keys, values, queries


def attend(first, weight, triple, probs, mixed, scalars, seqs):
    triple[...] = nn(first[...], weight[...]).astype(BF)
    base, starts, counts, lengths = scalars
    parts = [blocks_of(triple, s) for s in range(seqs)]
    for s, (keys, _, queries) in enumerate(parts):
        probs[s] = nt(keys, queries)
    for s in range(seqs):
        bias = mask_of(*(ref[base + s] for ref in (starts, counts, lengths)))
        for h in range(2):
            at = slice(h * SEQ, (h + 1) * SEQ)
            score = probs[s, at, :] + bias
            weights = jnp.exp(score - jnp.max(score, axis=0, keepdims=True))
            probs[s, at, :] = weights * (1.0 / jnp.sum(weights, axis=0, keepdims=True))
    for s, (_, values, _) in enumerate(parts):
        mixed[s * SEQ : (s + 1) * SEQ, :] = tn(probs[s].astype(BF), values).astype(BF)


def attend_back(middle_low, proj, triple, probs, seqs, gtl, grad_mixed, grad_probs):
    grad_mixed[...] = nn(middle_low[...], proj[: middle_low.shape[1], :]).astype(BF)
    parts = [blocks_of(triple, s) for s in range(seqs)]
    spots = [slice(s * SEQ, (s + 1) * SEQ) for s in range(seqs)]
    for s, (_, values, _) in enumerate(parts):
        grad_probs[s] = nt(values, grad_mixed[spots[s], :])
    lows = []
    for s in range(seqs):
        scores = []
        for h in range(2):
            at = slice(h * SEQ, (h + 1) * SEQ)
            prob, grad = probs[s, at, :], grad_probs[s, at, :]
            inner = jnp.sum(grad * prob, axis=0, keepdims=True)
            scores.append((prob * (grad - inner)).astype(BF))
        lows.append(jnp.concatenate(scores, 0))
    low = lanes_low((SEQ, 2 * HEAD_DIM))
    for s, (keys, _, queries) in enumerate(parts):
        grad_queries = half_turn(tn(lows[s], keys) * HEAD_DIM**-0.5)
        grad_keys = nn(lows[s], queries)
        grad_values = nn(probs[s].astype(BF), grad_mixed[spots[s], :])
        gtl[spots[s], 0:128] = jnp.where(low, grad_queries, grad_keys[:SEQ]).astype(BF)
        gtl[spots[s], 128:256] = jnp.where(low, grad_values[:SEQ], grad_queries).astype(BF)
        gtl[spots[s], 256:384] = jnp.where(low, grad_keys[SEQ:], grad_values[SEQ:]).astype(BF)


def gelu_parts(x):
    c0, c1 = 0.7978845608028654, 0.044715
    square = x * x
    t = jnp.tanh(x * (c0 + (c0 * c1) * square))
    h = 0.5 * (1.0 + t)
    slope = h + (0.5 * x) * (1.0 - t * t) * (c0 + (3.0 * c0 * c1) * square)
    return x * h, slope


def pack_kernel(proj, bias, place, base, out, *more):
    deep, span = proj.shape[1], out.shape[1]
    out[:deep, :] = proj[...].T
    rows = bias.shape[1] // span
    out[deep:, :] = jnp.concatenate(
        [bias[:, k * span : (k + 1) * span] for k in range(rows)]
        + [jnp.zeros((16 - rows, span), out.dtype)],
        0,
    )


def bundle_kernel(proj, bias, down, place, base, out, bundle):
    pack_kernel(proj, bias, place, base, out)
    deep, span = out.shape
    bundle[:deep, :] = out[...]
    half, per = down.shape[0] // 2, down.shape[1] // span
    rows = down[pl.ds(pl.multiple_of((place[0] % 2) * half, half), half), :]
    for k in range(per):
        bundle[deep + k * half : deep + (k + 1) * half, :] = rows[:, k * span : (k + 1) * span]


def unbundle_kernel(bundle, out, rows):
    deep, span = out.shape
    out[...] = bundle[:deep, :]
    half = rows.shape[0]
    for k in range(rows.shape[1] // span):
        rows[:, k * span : (k + 1) * span] = bundle[deep + k * half : deep + (k + 1) * half, :]


def pair_kernel(*refs):
    out, col = refs[-1], 0
    for part in refs[:-1]:
        out[:, col : col + part.shape[1]] = part[...]
        col += part.shape[1]


def relay_kernel(value, out):
    out[...] = value[...]


def attend_kernel(units, seqs, *refs):
    refs = list(refs)
    take = lambda n: [refs.pop(0) for _ in range(n)]
    (first,) = take(1)
    weights = take(units)
    scalars = take(4)
    scalars = [scalars[0][0]] + scalars[1:]
    triples, probs, mixeds = take(units), take(units), take(units)
    for u in range(units):
        attend(first, weights[u], triples[u], probs[u], mixeds[u], scalars, seqs)


def project_kernel(units, *refs):
    mixeds, projs, acc = refs[:units], refs[units : 2 * units], refs[2 * units]
    acc[...] = sum(
        nt(mixeds[u][...], projs[u][: acc.shape[1], :]) for u in range(units)
    )


def second_kernel(units, *refs):
    refs = list(refs)
    take = lambda n: [refs.pop(0) for _ in range(n)]
    mixeds, projs = take(units), take(units)
    acc, residual, bias, gain, shift, middle, second, second_t = refs
    for r in range(0, acc.shape[0], CHUNK):
        at = slice(r, r + CHUNK)
        out = acc[at, :] + sum(
            nt(mixeds[u][at, :], projs[u][: acc.shape[1], :]) for u in range(units)
        )
        out = residual[at, :] + out + bias[...]
        middle[at, :] = out
        xhat, _ = centred(out)
        low = (xhat * gain[...] + shift[...]).astype(BF)
        second[at, :] = low
        second_t[:, at] = low.T


def hidden_kernel(slots, *refs):
    refs = list(refs)
    take = lambda n: [refs.pop(0) for _ in range(n)]
    second, out_t = take(2)
    ups, biases = take(slots), take(slots)
    acts, slopes, grads = take(slots), take(slots), take(slots)
    for j in range(slots):
        span, tile = biases[j].shape[1], biases[j][second.shape[1] :, :].astype(F32)
        bias = jnp.concatenate([tile[k : k + 1, :] for k in range(ups[j].shape[1] // span)], 1)
        for r in range(0, second.shape[0], 2 * CHUNK):
            at = slice(r, r + 2 * CHUNK)
            act, slope = gelu_parts(nn(second[at, :], ups[j][...]) + bias)
            acts[j][at, :] = act.astype(BF)
            slopes[j][at, :] = slope
        grads[j][...] = nn(out_t[...], acts[j][...]).astype(grads[j].dtype)


def hidden_back_kernel(pieces, first_call, *refs):
    refs, slots = list(refs), len(pieces)
    take = lambda n: [refs.pop(0) for _ in range(n)]
    out_low, second_t = take(2)
    ups, downs, slopes = take(slots), take(slots), take(slots)
    acc_in = None if first_call else take(1)[0]
    grads, biases = [take(n) for n in pieces], take(slots)
    (acc,) = take(1)
    pre = take(slots)
    for j in range(slots):
        total = 0.0
        for r in range(0, out_low.shape[0], 2 * CHUNK):
            at = slice(r, r + 2 * CHUNK)
            low = (nt(out_low[at, :], downs[j][...]) * slopes[j][at, :]).astype(BF)
            pre[j][at, :] = low
            total = total + jnp.sum(low.astype(F32), axis=0, keepdims=True)
        biases[j][...] = total
        grad, first = nn(second_t[...], pre[j][...]), 0
        for out in grads[j]:
            out[...] = grad[first : first + out.shape[0], :].astype(out.dtype)
            first += out.shape[0]
    for r in range(0, out_low.shape[0], 2 * CHUNK):
        at = slice(r, r + 2 * CHUNK)
        out = sum(nt(pre[j][at, :], ups[j][...]) for j in range(slots))
        acc[at, :] = out if first_call else acc_in[at, :] + out


def middle_kernel(grad_second, middle, gain, cot, grad_middle, middle_low, middle_t, sums):
    totals = [0.0, 0.0, 0.0]
    for r in range(0, cot.shape[0], CHUNK):
        at = slice(r, r + CHUNK)
        row, dgain, dshift = norm_back(grad_second[at, :], middle[at, :], gain[...])
        grad = cot[at, :] + row
        grad_middle[at, :] = grad
        low = grad.astype(BF)
        middle_low[at, :] = low
        middle_t[:, at] = low.T
        parts = (jnp.sum(grad, axis=0, keepdims=True), dgain, dshift)
        totals = [t + p for t, p in zip(totals, parts)]
    for i, t in enumerate(totals):
        sums[i : i + 1, :] = t


def attend_back_kernel(units, group, pieces, seqs, *refs):
    refs = list(refs)
    take = lambda n: [refs.pop(0) for _ in range(n)]
    middle_low, middle_t, first_t = take(3)
    projs, triples, probs, mixeds = take(units), take(units), take(units), take(units)
    gtls, grads = take(units), [take(n) for n in pieces]
    grad_mixed, grad_probs = take(units), take(units)
    span, small = 6 * HEAD_DIM // group, 2 * HEAD_DIM // group
    for u in range(units):
        attend_back(
            middle_low,
            projs[u],
            triples[u],
            probs[u],
            seqs,
            gtls[u],
            grad_mixed[u],
            grad_probs[u],
        )
        grad = nn(first_t[...], gtls[u][...])
        proj_grad = nn(middle_t[...], mixeds[u][...])
        for k in range(group):
            first = 0
            for out in grads[u * group + k]:
                at = slice(first, first + out.shape[0])
                first += out.shape[0]
                out[:, :span] = grad[at, k * span : (k + 1) * span].astype(out.dtype)
                out[:, span:] = proj_grad[at, k * small : (k + 1) * small].astype(out.dtype)


def input_kernel(units, *refs):
    refs = list(refs)
    take = lambda n: [refs.pop(0) for _ in range(n)]
    gtls, weights = take(units), take(units)
    residual, gain, grad_middle, cot = take(4)
    grad_input, sums = take(2)
    totals = [0.0, 0.0, 0.0]
    for r in range(0, cot.shape[0], CHUNK):
        at = slice(r, r + CHUNK)
        grad = sum(nt(gtls[u][at, :], weights[u][...]) for u in range(units))
        row, dgain, dshift = norm_back(grad, residual[at, :], gain[...])
        grad_input[at, :] = grad_middle[at, :] + row
        parts = (jnp.sum(cot[at, :], axis=0, keepdims=True), dgain, dshift)
        totals = [t + p for t, p in zip(totals, parts)]
    for i, t in enumerate(totals):
        sums[i : i + 1, :] = t


def output_kernel(slots, *refs):
    acts, downs = refs[:slots], refs[slots : 2 * slots]
    middle, bias, out = refs[2 * slots :]
    for r in range(0, middle.shape[0], 2 * CHUNK):
        at = slice(r, r + 2 * CHUNK)
        total = sum(nn(acts[j][at, :], downs[j][...]) for j in range(slots))
        out[at, :] = middle[at, :] + total + bias[...]


def total(terms):
    out = terms[0]
    for term in terms[1:]:
        out = out + term
    return out


def read(refs, spots, at):
    terms = []
    for where, first in spots:
        if len(where) > 1:
            terms.append(jnp.concatenate([refs[i][...] for i in where], 0).astype(F32))
        else:
            terms.append(refs[where[0]][pl.ds(first + at[0], at[1]), :].astype(F32))
    return total(terms)


def rider_rows(rider, cols):
    return 2 * rider[0] * -(-(rider[1] // 128) // max(1, cols // 128))


def pack_rider(rider, out, first):
    per, deep = max(1, out.shape[1] // 128), 2 * rider.shape[0]
    high = rider.astype(BF)
    rest = (rider - high.astype(F32)).astype(BF)
    for j in range(rider.shape[1] // 128):
        at, row, col = slice(j * 128, (j + 1) * 128), first + deep * (j // per), 128 * (j % per)
        block = jnp.concatenate([high[:, at], rest[:, at]], 0)
        out[row : row + deep, col : col + 128] = block


def unpack_rider(value, first, shape):
    rows, per, parts = shape[0], max(1, value.shape[1] // 128), []
    for j in range(shape[1] // 128):
        row, col = first + 2 * rows * (j // per), 128 * (j % per)
        block = value[row : row + 2 * rows, col : col + 128].astype(F32)
        parts.append(block[:rows, :] + block[rows:, :])
    return jnp.concatenate(parts, 1)


def rider_total(refs, ride):
    kept, came, first = ride
    rider = refs[kept][...]
    for i in came:
        rider = rider + unpack_rider(refs[i], first, rider.shape)
    return rider


def send_kernel(spots, rows, *refs):
    count = 1 + max(i for spot in spots for where, _ in spot for i in where)
    outs = refs[count:]
    if len(outs) > 1:
        value = read(refs, spots[0], (0, rows)).astype(BF)
        for k, out in enumerate(outs):
            out[...] = value[k * out.shape[0] : (k + 1) * out.shape[0], :]
        return
    (out,) = outs
    used = len(spots) * rows
    for k, spot in enumerate(spots):
        out[k * rows : (k + 1) * rows, :] = read(refs, spot, (0, rows)).astype(out.dtype)
    if used < out.shape[0]:
        out[used:, :] = jnp.zeros((out.shape[0] - used, out.shape[1]), out.dtype)


def halve_kernel(spots, rows, bit, ride, *refs):
    refs = list(refs)
    if ride:
        rider_keep = refs.pop()
    send = refs.pop()
    stays = [refs.pop() for _ in spots][::-1]
    place = refs.pop()
    half = rows // 2
    mine = (place[0] // bit) % 2
    for k, spot in enumerate(spots):
        stays[k][...] = read(refs, spot, (pl.multiple_of(mine * half, half), half))
        leave = read(refs, spot, (pl.multiple_of((1 - mine) * half, half), half))
        send[k * half : (k + 1) * half, :] = leave.astype(BF)
    room = len(spots) * half
    if room < send.shape[0]:
        send[room:, :] = jnp.zeros((send.shape[0] - room, send.shape[1]), BF)
    if ride:
        rider = rider_total(refs, ride)
        rider_keep[...] = rider
        pack_rider(rider, send, len(spots) * half)


def whole_kernel(spots, rows, ride, *refs):
    refs = list(refs)
    if ride:
        rider_keep = refs.pop()
    send, keep = refs.pop(), refs.pop()
    value = read(refs, spots[0], (0, rows))
    keep[...] = value
    send[:rows, :] = value.astype(BF)
    send[rows:, :] = jnp.zeros((send.shape[0] - rows, send.shape[1]), BF)
    if ride:
        rider = rider_total(refs, ride)
        rider_keep[...] = rider
        pack_rider(rider, send, rows)


def settle_kernel(spots, rows, ride, *refs):
    refs = list(refs)
    if ride:
        rider_out = refs.pop()
    out = refs.pop()
    out[...] = read(refs, spots[0], (0, rows)).astype(out.dtype)
    if ride:
        rider_out[...] = rider_total(refs, ride)


def join_kernel(bit, own, other, place, out):
    half = own.shape[0]
    mine = (place[0] // bit) % 2
    out[pl.ds(pl.multiple_of(mine * half, half), half), :] = own[...].astype(out.dtype)
    out[pl.ds(pl.multiple_of((1 - mine) * half, half), half), :] = other[...].astype(out.dtype)


def finish_kernel(bit, blocks, turned, own, other, place, *refs):
    outs, low = refs[:-1], refs[-1]
    join_kernel(bit, own, other, place, low)
    rows, col = low.shape[0] // len(blocks), 0
    for out, turn in zip(outs, turned):
        span = out.shape[0] if turn else out.shape[1]
        for to, at in enumerate(blocks):
            part = low[at * rows : (at + 1) * rows, col : col + span]
            if turn:
                out[:, to * rows : (to + 1) * rows] = part.T
            else:
                out[to * rows : (to + 1) * rows, :] = part
        col += span


def vector_kernel(parts, *refs):
    out = refs[-1]
    out[...] = jnp.zeros_like(out)
    row = 0
    for ref, n in zip(refs, parts):
        out[row : row + n, : ref.shape[1]] = ref[:n, :]
        row += n


def vector_core_kernel(heads, fixed, mine, got, out):
    out[...] = jnp.zeros_like(out)
    out[:fixed, :] = mine[:fixed, :] + got[:fixed, :]
    for k in range(0, heads, 2):
        at, other, to = fixed + k, fixed + k + 1, fixed + k // 2
        out[to : to + 1, :] = mine[at : at + 1, :] + got[other : other + 1, :]


def vector_add_kernel(bit, fixed, mine, got, out):
    out[...] = mine[...] + got[...]
    for k in range(out.shape[0] - fixed):
        if k ^ bit < out.shape[0] - fixed:
            at, other = fixed + k, fixed + (k ^ bit)
            out[at : at + 1, :] = mine[at : at + 1, :] + got[other : other + 1, :]


def vector_last_kernel(bit, fixed, mine, got, *outs):
    for k in range(fixed + 1):
        other, span = (k if k < fixed else fixed + bit), outs[k].shape[1]
        outs[k][...] = mine[k : k + 1, :span] + got[other : other + 1, :span]


class Links:
    def __init__(self, mesh):
        self.dp, self.head = mesh.shape["dp"], mesh.shape["head"]

    def swap(self, value, bit):
        total = self.dp * self.head
        return lax.ppermute(value, AXES, [(i, i ^ bit) for i in range(total)])


class Chain:
    def __init__(self, links, kernels, place, room, tag):
        self.tag = tag
        self.room = room
        self.links, self.kernels, self.place = links, kernels, place
        self.slots, self.bit, self.halved = {}, 2, []
        self.rider, self.rider_came = None, []
        self.rider_first = 0

    def give(self, slot, *values):
        self.rows, self.cols = sum(v.shape[0] for v in values), values[0].shape[1]
        if slot % 2:
            got = [self.links.swap(v, 1) for v in values]
            self.slots.setdefault(slot - 1, []).insert(0, (got, 0))
        else:
            self.slots.setdefault(slot, []).insert(0, (list(values), 0))

    def give_later(self, slot, value):
        (value,) = self.kernels.call(relay_kernel, [(value.shape, BF)], value, name="relay")
        self.give(slot, value)

    def spots(self, sums):
        arrays, spots = [], []
        for terms in sums:
            spots.append([])
            for values, first in terms:
                where = []
                for value in values:
                    known = [i for i, a in enumerate(arrays) if a is value]
                    if not known:
                        arrays.append(value)
                        known = [len(arrays) - 1]
                    where.append(known[0])
                spots[-1].append((where, first))
        return arrays, spots

    def head(self, pieces=1, spare=False):
        leave = [k for k in self.slots if k & self.bit]
        arrays, spots = self.spots([self.slots[k] for k in leave])
        room = rider_rows(self.room, self.cols) if self.halved or spare else 0
        deep = len(leave) * self.rows + room
        sends = self.kernels.call(
            functools.partial(send_kernel, spots, self.rows),
            [((deep // pieces, self.cols), BF)] * pieces,
            *arrays,
            name="send_" + self.tag,
        )
        got = [self.links.swap(send, self.bit) for send in sends]
        for i, k in enumerate(leave):
            del self.slots[k]
            self.slots.setdefault(k ^ self.bit, []).append((got, i * self.rows))
        self.bit *= 2

    def fold(self, slot, count=2):
        arrays, spots = self.spots([self.slots[slot][:count]])
        (value,) = self.kernels.call(
            functools.partial(send_kernel, spots, self.rows),
            [((self.rows, self.cols), F32)],
            *arrays,
            name="fold_" + self.tag,
        )
        self.slots[slot][:count] = [([value], 0)]

    def ride(self, arrays):
        if self.rider is None:
            return None
        arrays.append(self.rider)
        came = [i for i, a in enumerate(arrays) if any(a is b for b in self.rider_came)]
        return len(arrays) - 1, came, self.rider_first

    def rode(self, kept, came, first):
        if self.rider is not None:
            self.rider, self.rider_came, self.rider_first = kept, came, first

    def halve(self, bit):
        keys = list(self.slots)
        arrays, spots = self.spots([self.slots[k] for k in keys])
        half = self.rows // 2
        ride = self.ride(arrays)
        rider = [(self.rider.shape, F32)] if ride else []
        more = rider_rows(self.room, self.cols) if self.halved or len(keys) == 1 else 0
        got = self.kernels.call(
            functools.partial(halve_kernel, spots, self.rows, bit, ride),
            [((half, self.cols), F32)] * len(keys)
            + [((len(keys) * half + more, self.cols), BF)]
            + rider,
            *arrays,
            self.place,
            scalars=1,
            name="halve_" + self.tag,
        )
        came = self.links.swap(got[len(keys)], bit * self.links.head)
        self.slots = {k: [([got[i]], 0), ([came], i * half)] for i, k in enumerate(keys)}
        self.rode(got[-1], [came], len(keys) * half)
        self.rows = half
        self.halved.append(bit)

    def whole(self, bit):
        arrays, spots = self.spots([self.slots[0]])
        ride = self.ride(arrays)
        rider = [(self.rider.shape, F32)] if ride else []
        more = rider_rows(self.room, self.cols)
        got = self.kernels.call(
            functools.partial(whole_kernel, spots, self.rows, ride),
            [((self.rows, self.cols), F32), ((self.rows + more, self.cols), BF)] + rider,
            *arrays,
            name="whole_" + self.tag,
        )
        came = self.links.swap(got[1], bit * self.links.head)
        self.slots = {0: [([got[0]], 0), ([came], 0)]}
        self.rode(got[-1], [came], self.rows)

    def settle(self, order):
        arrays, spots = self.spots([self.slots[0]])
        ride = self.ride(arrays)
        got = self.kernels.call(
            functools.partial(settle_kernel, spots, self.rows, ride),
            [((self.rows, self.cols), BF)] + ([(self.rider.shape, F32)] if ride else []),
            *arrays,
            name="settle_" + self.tag,
        )
        self.own, self.order, self.left = got[0], list(order), list(order)
        self.back()
        return got[-1]

    def back(self):
        self.last = self.left.pop(0)
        self.got = self.links.swap(self.own, self.last * self.links.head)

    def double(self):
        if not self.left:
            return
        self.rows *= 2
        (self.own,) = self.kernels.call(
            functools.partial(join_kernel, self.last),
            [((self.rows, self.cols), BF)],
            self.own,
            self.got,
            self.place,
            scalars=1,
            name="join_" + self.tag,
        )
        self.back()

    def finish(self, outs, turned):
        blocks = []
        for to in range(2 ** len(self.order)):
            digits = {b: to >> (len(self.halved) - 1 - i) & 1 for i, b in enumerate(self.halved)}
            blocks.append(sum(digits[b] << i for i, b in enumerate(self.order)))
        if blocks == sorted(blocks):
            blocks = [0]
        return self.kernels.call(
            functools.partial(finish_kernel, self.last, blocks, turned),
            [(o, F32, True) for o in outs],
            self.own,
            self.got,
            self.place,
            scalars=1,
            scratch=[((2 * self.rows, self.cols), F32)],
            name="finish_" + self.tag,
        )


def make(mesh):
    links = Links(mesh)
    nslots = links.head
    bits = [2**k for k in range(links.dp.bit_length() - 1)]

    def shards(
        residual_in,
        cotangent,
        triple_weight,
        proj_weight,
        up_weight,
        up_bias,
        down_weight,
        proj_bias,
        down_bias,
        first_gain,
        first_shift,
        second_gain,
        second_shift,
        start_steps,
        cond_counts,
        valid_lengths,
    ):
        kernels = Kernels()
        call = kernels.call
        rows, width = residual_in.shape
        seqs = rows // SEQ
        hidden, proj_rows = up_weight.shape[1], proj_weight.shape[0]
        row = lambda v: v.reshape(1, -1)
        proj_bias, down_bias, first_gain, first_shift, second_gain, second_shift = map(
            row, (proj_bias, down_bias, first_gain, first_shift, second_gain, second_shift)
        )
        place = lax.axis_index("dp").astype(jnp.int32).reshape(1)
        base = (lax.axis_index("head") * seqs).astype(jnp.int32).reshape(1)
        scalars = (base, start_steps, cond_counts, valid_lengths)
        group = 2 * HEAD_DIM // proj_rows
        units = nslots // group

        slots = {}

        def far(key, value):
            known = {0: value}
            bit = nslots // 2
            while bit > 1:
                known.update({k | bit: links.swap(v, bit) for k, v in list(known.items())})
                bit //= 2
            slots[key] = known

        def near(key):
            slots[key][1] = links.swap(slots[key][0], 1)

        def relay(key, k):
            value = slots[key][k]
            (value,) = call(relay_kernel, [(value.shape, BF)], value, name="relay")
            slots[key][k + 1] = links.swap(value, 1)

        far("t", triple_weight)
        near("t")
        far("u", up_weight)
        near("u")
        slots["d"] = {0: down_weight, 1: links.swap(down_weight, 1)}
        shared = nslots == 4 and len(bits) > 1
        pack_shape = (width + 16, proj_rows)
        half = (down_weight.shape[0] // 2, width)
        evens, odds = range(2, nslots, 2), range(3, nslots, 2)
        early = list(range(max(1, 2 // group)))
        late = [u for u in range(units) if u not in early]
        triple_w, proj_w, triples, probs, mixeds = {}, {}, {}, {}, {}
        acts, slopes, biases, down_grads, up_grads = {}, {}, {}, {}, {}
        gtls, triple_grads = {}, {}
        room = (8 * -(-(6 + nslots // 2) // 8), width)
        down_sum, up_sum, triple_sum = (Chain(links, kernels, place, room, t) for t in "dut")
        middle_bits, there = bits[1:-1], bits[:-1]
        s = types.SimpleNamespace()
        thirds = [width // 48 * 16 + 16] * 2
        thirds = thirds + [width - sum(thirds)]

        def kind(k):
            return BF if k % 2 else F32

        def bundle():
            if shared:
                deep = pack_shape[0] + half[0] * width // proj_rows
                packed, sent = call(
                    bundle_kernel,
                    [(pack_shape, BF), ((deep, proj_rows), BF)],
                    proj_weight,
                    row(up_bias),
                    down_weight,
                    place,
                    base,
                    scalars=2,
                    name="bundle",
                )
                s.bundle = links.swap(sent, 2)
                slots["p"] = {0: packed, 1: links.swap(packed, 1)}
                return
            (packed,) = call(
                pack_kernel,
                [(pack_shape, BF)],
                proj_weight,
                row(up_bias),
                place,
                base,
                scalars=2,
                name="pack",
            )
            far("p", packed)
            near("p")
            far("d", down_weight)
            near("d")

        def prep():
            s.first, s.first_t = call(
                prep_kernel,
                [((rows, width), BF), ((width, rows), BF)],
                residual_in,
                first_gain,
                first_shift,
                also=[slots["u"][1], slots["d"][1]],
                name="prep",
            )

        def attend_call(which):
            n = len(which)
            for u in which:
                parts = [slots["t"][k] for k in range(u * group, (u + 1) * group)]
                triple_w[u] = parts[0]
                if group > 1:
                    (triple_w[u],) = call(
                        pair_kernel, [((width, 6 * HEAD_DIM), BF)], *parts, name="pair"
                    )
            got = call(
                functools.partial(attend_kernel, n, seqs),
                [((rows, 6 * HEAD_DIM), BF)] * n
                + [((seqs, 2 * SEQ, SEQ), F32)] * n
                + [((rows, 2 * HEAD_DIM), BF)] * n,
                s.first,
                *(triple_w[u] for u in which),
                *scalars,
                scalars=4,
                name="attend",
            )
            for i, u in enumerate(which):
                triples[u], probs[u], mixeds[u] = got[i], got[n + i], got[2 * n + i]

        def project_rows(which):
            for u in which:
                parts = [slots["p"][k] for k in range(u * group, (u + 1) * group)]
                proj_w[u] = parts[0]
                if group > 1:
                    (proj_w[u],) = call(
                        pair_kernel, [((width + 16, 2 * HEAD_DIM), BF)], *parts, name="pair"
                    )

        def cot_low():
            s.out_low, s.out_t = call(
                out_kernel, [((rows, width), BF), ((width, rows), BF)], cotangent, name="out"
            )

        def project():
            project_rows(early)
            (s.acc,) = call(
                functools.partial(project_kernel, len(early)),
                [((rows, width), F32)],
                *(mixeds[u] for u in early),
                *(proj_w[u] for u in early),
                name="project",
            )

        def relay_triple():
            for k in evens:
                relay("t", k)

        def unbundle():
            if shared:
                slots["p"][2], s.half_low = call(
                    unbundle_kernel, [(pack_shape, BF), (half, BF)], s.bundle, name="unbundle"
                )
                slots["p"][3] = links.swap(slots["p"][2], 1)
                s.down_other = links.swap(s.half_low, nslots)
                return
            for k in evens:
                relay("p", k)

        def second():
            project_rows(late)
            s.middle, s.second, s.second_t = call(
                functools.partial(second_kernel, len(late)),
                [((rows, width), F32), ((rows, width), BF), ((width, rows), BF)],
                *(mixeds[u] for u in late),
                *(proj_w[u] for u in late),
                s.acc,
                residual_in,
                proj_bias,
                second_gain,
                second_shift,
                name="second",
            )

        def hidden_call(which):
            n = len(which)
            got = call(
                functools.partial(hidden_kernel, n),
                [((rows, hidden), BF)] * n
                + [((rows, hidden), F32)] * n
                + [((width, hidden), kind(k)) for k in which],
                s.second,
                s.out_t,
                *(slots["u"][k] for k in which),
                *(slots["p"][k] for k in which),
                name="hidden",
            )
            for i, k in enumerate(which):
                acts[k], slopes[k], down_grads[k] = got[i], got[n + i], got[2 * n + i]
                if k != 1:
                    down_sum.give(k, down_grads[k])

        def hidden_back_call(which):
            n, acc = len(which), [s.grad_second] if hasattr(s, "grad_second") else []
            pieces = [thirds if k % 2 and k > 1 else [width] for k in which]
            got = call(
                functools.partial(hidden_back_kernel, [len(p) for p in pieces], not acc),
                [((r, hidden), kind(k)) for k, p in zip(which, pieces) for r in p]
                + [((1, hidden), F32)] * n
                + [((rows, width), F32)],
                s.out_low,
                s.second_t,
                *(slots["u"][k] for k in which),
                *(slots["d"][k] for k in which),
                *(slopes[k] for k in which),
                *acc,
                scratch=[((rows, hidden), BF)] * n,
                name="hidden_back",
            )
            got = list(got)
            for k, p in zip(which, pieces):
                up_grads[k] = [got.pop(0) for _ in p]
                if k != 1:
                    up_sum.give(k, *up_grads[k])
            for k in which:
                biases[k] = got.pop(0)
            s.grad_second = got.pop(0)

        def join_down():
            if shared:
                (slots["d"][2],) = call(
                    functools.partial(join_kernel, 1),
                    [(down_weight.shape, BF)],
                    s.half_low,
                    s.down_other,
                    place,
                    scalars=1,
                    name="join",
                )
                slots["d"][3] = links.swap(slots["d"][2], 1)
                return
            for k in evens:
                relay("d", k)

        def relay_up():
            for k in evens:
                relay("u", k)

        def middle():
            s.grad_middle, s.middle_low, s.middle_t, s.sums_middle = call(
                middle_kernel,
                [((rows, width), F32), ((rows, width), BF), ((width, rows), BF), ((8, width), F32)],
                s.grad_second,
                s.middle,
                second_gain,
                cotangent,
                name="middle",
            )

        def attend_back_call(which):
            n = len(which)
            which_slots = [k for u in which for k in range(group * u, group * (u + 1))]
            pieces = [thirds if k % 2 and k > 1 else [width] for k in which_slots]
            span = 8 * HEAD_DIM // group
            got = call(
                functools.partial(attend_back_kernel, n, group, [len(p) for p in pieces], seqs),
                [((rows, 6 * HEAD_DIM), BF)] * n
                + [((r, span), kind(k)) for k, p in zip(which_slots, pieces) for r in p],
                s.middle_low,
                s.middle_t,
                s.first_t,
                *(proj_w[u] for u in which),
                *(triples[u] for u in which),
                *(probs[u] for u in which),
                *(mixeds[u] for u in which),
                scratch=[((rows, 2 * HEAD_DIM), BF)] * n + [((seqs, 2 * SEQ, SEQ), F32)] * n,
                name="attend_back",
            )
            for i, u in enumerate(which):
                gtls[u] = got[i]
            got = list(got[n:])
            for k, p in zip(which_slots, pieces):
                triple_sum.give(k, *(got.pop(0) for _ in p))

        def heads(chain, spare=False):
            while chain.bit < nslots:
                chain.head(spare=spare)

        def input_grad():
            s.grad_input, s.sums_input = call(
                functools.partial(input_kernel, units),
                [((rows, width), F32, True), ((8, width), F32)],
                *(gtls[u] for u in range(units)),
                *(triple_w[u] for u in range(units)),
                residual_in,
                first_gain,
                s.grad_middle,
                cotangent,
                name="input",
            )

        def vector():
            (s.vector,) = call(
                functools.partial(vector_kernel, [3, 3] + [1] * nslots),
                [((16, width), F32)],
                s.sums_middle,
                s.sums_input,
                *(biases[k] for k in range(nslots)),
                name="vector",
            )
            s.vector_got = links.swap(s.vector, 1)

        def vector_core():
            (triple_sum.rider,) = call(
                functools.partial(vector_core_kernel, nslots, 6),
                [(room, F32)],
                s.vector,
                s.vector_got,
                name="vector_core",
            )

        def halves(chain):
            for bit in middle_bits:
                chain.halve(bit)

        def block():
            (s.block_out,) = call(
                functools.partial(output_kernel, nslots),
                [((rows, width), F32, True)],
                *(acts[k] for k in range(nslots)),
                *(slots["d"][k] for k in range(nslots)),
                s.middle,
                down_bias,
                name="output",
            )

        def settle(chain, order=None):
            chain.settle(order or there[::-1])
            for _ in there[2:]:
                chain.double()

        def settle_triple():
            s.vector = triple_sum.settle(there[::-1])
            for _ in there[2:]:
                triple_sum.double()
            s.vector_bit = 2
            s.vector_got = links.swap(s.vector, 2)

        def finish_triple():
            outs = [(width, 6 * HEAD_DIM // group), (proj_rows, width)], [False, True]
            s.grad_triple, s.grad_proj = triple_sum.finish(*outs)

        def totals():
            while 2 * s.vector_bit < nslots:
                (s.vector,) = call(
                    functools.partial(vector_add_kernel, s.vector_bit // 2, 6),
                    [(room, F32)],
                    s.vector,
                    s.vector_got,
                    name="vector_add",
                )
                s.vector_bit *= 2
                s.vector_got = links.swap(s.vector, s.vector_bit)
            s.totals = call(
                functools.partial(vector_last_kernel, s.vector_bit // 2, 6),
                [((1, width), F32)] * 6 + [((1, hidden), F32)],
                s.vector,
                s.vector_got,
                name="vector_last",
            )

        def finish_down():
            (s.grad_down,) = down_sum.finish([(hidden, width)], [True])

        def finish_up():
            (s.grad_up,) = up_sum.finish([(width, hidden)], [False])

        bundle()
        prep()
        attend_call(early)
        cot_low()
        project()
        relay_triple()
        for u in late:
            attend_call([u])
        unbundle()
        second()
        hidden_call([0, 1])
        join_down()
        hidden_back_call([0, 1])
        down_sum.give_later(1, down_grads[1])
        relay_up()
        up_sum.give_later(1, *up_grads[1])
        down_sum.fold(0)
        for k in odds:
            hidden_call([k])
        for k in odds:
            hidden_back_call([k])
        for k in evens:
            hidden_call([k])
        up_sum.fold(0)
        heads(down_sum, True)
        for k in evens:
            hidden_back_call([k])
        middle()
        for k in evens:
            up_sum.fold(k)
        up_sum.halve(bits[0])
        attend_back_call(late[::-1])
        attend_back_call(early[::-1])
        heads(triple_sum)
        input_grad()
        heads(up_sum)
        down_sum.halve(bits[0])
        vector()
        halves(down_sum)
        vector_core()
        triple_sum.halve(bits[0])
        halves(up_sum)
        halves(triple_sum)
        down_sum.whole(bits[-1])
        triple_sum.whole(bits[-1])
        block()
        settle(down_sum, there)
        up_sum.whole(bits[-1])
        settle_triple()
        settle(up_sum, there)
        down_sum.double()
        triple_sum.double()
        up_sum.double()
        finish_down()
        totals()
        finish_triple()
        finish_up()
        totals = [v.reshape(-1) for v in s.totals]
        return (
            s.block_out,
            s.grad_input,
            s.grad_triple,
            s.grad_proj,
            s.grad_up,
            totals[6],
            s.grad_down,
            totals[0],
            totals[3],
            totals[4],
            totals[5],
            totals[1],
            totals[2],
        )

    return shards


def solution(mesh):
    in_specs = (
        P(("dp", "head"), None),
        P(("dp", "head"), None),
        P(None, "head"),
        P("head", None),
        P(None, "head"),
        P("head"),
        P("head", None),
        P(),
        P(),
        P(),
        P(),
        P(),
        P(),
        P("dp"),
        P("dp"),
        P("dp"),
    )
    out_specs = (
        P(("dp", "head"), None),
        P(("dp", "head"), None),
        P(None, "head"),
        P("head", None),
        P(None, "head"),
        P("head"),
        P("head", None),
        P(),
        P(),
        P(),
        P(),
        P(),
        P(),
    )
    return jax.shard_map(
        make(mesh), mesh=mesh, in_specs=in_specs, out_specs=out_specs, check_vma=False
    )
```
